256 devices in a mesh: dp: 16 (over z, x_lo), mp: 16 (over y, x_hi, core).
Axes of the slice: x: 4 (x_hi: 2, x_lo: 2; x = x_hi * 2 + x_lo), y: 4, z: 8, core: 2. Of those that a mesh axis runs over, the one named last changes fastest.
Arguments:
- tokens: bfloat16 [4096, 8192], P('dp', 'mp'), may hold values from -6 to 6
- cotangent: bfloat16 [4096, 8192], P('dp', 'mp'), may hold values from -6 to 6
- w_in: bfloat16 [64, 4, 256, 256], P('mp'), may hold values from -0.1875 to 0.1875
- w_out: bfloat16 [64, 4, 256, 256], P('mp'), may hold values from -0.125 to 0.125
- in_blocks: int32 [64, 4], P('mp'), may hold values from 0 to 31, as said below
- out_blocks: int32 [64, 4], P('mp'), may hold values from 0 to 31, as said below
Outputs:
- output: bfloat16 [4096, 8192], P('dp', 'mp')
- grad_tokens: bfloat16 [4096, 8192], P('dp', 'mp')
- grad_in: float32 [64, 4, 256, 256], P('mp', None, 'dp')
- grad_out: float32 [64, 4, 256, 256], P('mp', None, 'dp')
The draws below stay inside these ranges and needn't reach their ends.
Inputs may be any that keep to these rules, and one draw needn't show every extreme that they name: `in_blocks`: flat butterfly pattern: row j holds p(j mod 32 XOR m) for m = 0, 1, 2, 4, with p a permutation of the 32 input blocks; the 4 entries of a row differ and every block is named by exactly 8 rows. `out_blocks`: the same flat butterfly form with its own permutation q of the 32 output blocks.
All inputs are finite; a program needn't handle non-finite values.
Results may differ from the reference program's by a relative error of at most 0.018.
Values may be sent and summed in bfloat16 or wider, within the bound.
No kernel may reach another device: no remote copies, remote signals or barrier semaphores. Data moves between devices by JAX's collectives and lax.ppermute only.
A program may use at most 128 MiB of HBM per device.

```python
import jax
import jax.numpy as jnp
from jax import lax

D = 8192
BS = 256
K = 4
RB = 32
HB = 64
TOKENS = 4096
N_MP = 16


def butterfly_lists(key, salt):
    order = jax.random.permutation(jax.random.fold_in(key, salt), RB).astype(jnp.int32)
    base = jnp.arange(HB, dtype=jnp.int32) % RB
    masks = jnp.array([0, 1, 2, 4], dtype=jnp.int32)
    return order[jnp.bitwise_xor(base[:, None], masks[None, :])].astype(jnp.int32)


def draw_in_blocks(key, part):
    return butterfly_lists(key, 11)


def draw_out_blocks(key, part):
    return butterfly_lists(key, 23)


def block_scale(rng, shape, split, smallest, largest):
    level, own = 1.0, jax.random.fold_in(rng, 6)
    for position, shards_of in split:
        heights = jnp.exp(jax.random.uniform(jax.random.fold_in(own, position), (shards_of,), jnp.float32, smallest / len(split), largest / len(split)))
        level = level * jnp.repeat(heights, shape[position] // shards_of).reshape([-1 if axis == position else 1 for axis in range(len(shape))])
    return level


def gaussian(key, shape, width, limit, pieces=(), held_as=jnp.bfloat16):
    result = width * jax.random.normal(key, shape, jnp.float32)
    if pieces:
        result = result * block_scale(key, shape, pieces, -0.22, 0.18)
    return jnp.clip(result, -limit, limit).astype(held_as)


def setup_inputs(seed: int = 0) -> dict:
    streams_of = jax.random.split(jax.random.key(seed), 7)
    tokens = gaussian(streams_of[0], (TOKENS, D), 1.0, 6.0, ((0, 16), (1, 16)))
    cotangent = gaussian(streams_of[1], (TOKENS, D), 1.0, 6.0, ((0, 16), (1, 16)))
    w_in = gaussian(streams_of[2], (HB, K, BS, BS), (K * BS) ** -0.5, 0.1875, ((0, 16),))
    w_out = gaussian(streams_of[3], (HB, K, BS, BS), (HB * K * BS // RB) ** -0.5, 0.125, ((0, 16),))
    in_blocks = draw_in_blocks(jax.random.fold_in(streams_of[6], 71), 0)
    out_blocks = draw_out_blocks(jax.random.fold_in(streams_of[6], 71), 0)
    return dict(tokens=tokens, cotangent=cotangent, w_in=w_in, w_out=w_out, in_blocks=in_blocks, out_blocks=out_blocks)


def reference(tokens, cotangent, w_in, w_out, in_blocks, out_blocks):
    total = tokens.shape[0]
    group_size = HB // N_MP
    token_blocks = tokens.reshape(total, RB, BS)
    cot_blocks = cotangent.reshape(total, RB, BS)
    w_in_g = w_in.reshape(N_MP, group_size, K, BS, BS)
    w_out_g = w_out.reshape(N_MP, group_size, K, BS, BS)
    in_g = in_blocks.reshape(N_MP, group_size, K).astype(jnp.int32)
    out_g = out_blocks.reshape(N_MP, group_size, K).astype(jnp.int32)

    def group(carry, items):
        out_acc, back_acc = carry
        weight_in, weight_out, idx_in, idx_out = items
        selected = token_blocks[:, idx_in].astype(jnp.float32)
        pre = jnp.einsum('tjkb,jkbc->tjc', selected, weight_in.astype(jnp.float32))
        act = jax.nn.gelu(pre).astype(jnp.bfloat16)
        terms = jnp.einsum('tjb,jkbc->tjkc', act.astype(jnp.float32), weight_out.astype(jnp.float32))
        part = jnp.zeros((total, RB, BS), jnp.float32).at[:, idx_out.reshape(-1)].add(terms.reshape(total, group_size * K, BS))
        part = lax.optimization_barrier(part.reshape(total, D).astype(jnp.bfloat16)).astype(jnp.float32)
        picked = cot_blocks[:, idx_out].astype(jnp.float32)
        d_act = jnp.einsum('tjkc,jkbc->tjb', picked, weight_out.astype(jnp.float32))
        _, pullback = jax.vjp(jax.nn.gelu, pre)
        d_pre = pullback(d_act)[0].astype(jnp.bfloat16)
        grad_o = jnp.einsum('tjb,tjkc->jkbc', act.astype(jnp.float32), picked)
        grad_i = jnp.einsum('tjkb,tjc->jkbc', selected, d_pre.astype(jnp.float32))
        back = jnp.einsum('tjc,jkbc->tjkb', d_pre.astype(jnp.float32), weight_in.astype(jnp.float32))
        back_part = jnp.zeros((total, RB, BS), jnp.float32).at[:, idx_in.reshape(-1)].add(back.reshape(total, group_size * K, BS))
        back_part = lax.optimization_barrier(back_part.reshape(total, D).astype(jnp.bfloat16)).astype(jnp.float32)
        return ((out_acc + part, back_acc + back_part), (grad_i, grad_o))
    start = (jnp.zeros((total, D), jnp.float32), jnp.zeros((total, D), jnp.float32))
    (out_acc, back_acc), (grads_i, grads_o) = lax.scan(group, start, (w_in_g, w_out_g, in_g, out_g))
    scale = 1.0 / jnp.sqrt(jnp.float32(TOKENS))
    grad_in = grads_i.reshape(HB, K, BS, BS) * scale
    grad_out = grads_o.reshape(HB, K, BS, BS) * scale
    return (out_acc.astype(jnp.bfloat16), back_acc.astype(jnp.bfloat16), grad_in, grad_out)
```

```python
import functools
import math

import jax
import jax.numpy as jnp
from jax import lax
from jax.experimental import pallas as pl
from jax.experimental.pallas import tpu as pltpu
from jax.sharding import PartitionSpec as P

SIDE = 256
QUAD = 4 * SIDE
SLICE = 16
VMEM = pl.BlockSpec(memory_space=pltpu.VMEM)
SMEM = pl.BlockSpec(memory_space=pltpu.SMEM)
BF16 = jnp.bfloat16
F32 = jnp.float32


def params():
    return pltpu.CompilerParams(vmem_limit_bytes=48 * 1024 * 1024)


def pack_kernel(n, x_ref, dy_ref, p_ref, q_ref, out_ref):
    lane = lax.broadcasted_iota(jnp.int32, (2 * SLICE, 128), 1)
    lists = jnp.zeros((2 * SLICE, 128), F32)
    for t in range(4):
        lists = jnp.where(lane == t, p_ref[t, 0].astype(F32), lists)
        lists = jnp.where(lane == t + 4, q_ref[t, 0].astype(F32), lists)
    lists = lists.astype(BF16)
    for i in range(n):
        out_ref[i, :SLICE, : 2 * SIDE] = x_ref[pl.ds(i * SLICE, SLICE), :]
        out_ref[i, SLICE:, : 2 * SIDE] = dy_ref[pl.ds(i * SLICE, SLICE), :]
        out_ref[i, :, 2 * SIDE :] = lists


def select_kernel(n, got_ref, out_ref, lists_ref, table, sem):
    lists = jnp.max(got_ref[:, :SLICE, 2 * SIDE :].astype(F32), axis=1).astype(jnp.int32)
    lists_ref[...] = lists
    copy = pltpu.make_async_copy(lists_ref, table, sem)
    copy.start()
    copy.wait()
    for quad in range(n // 2):
        for t in range(4):
            for row, column in ((0, t), (SLICE, t + 4)):
                block = table[quad, column]
                owner = lax.shift_right_logical(block, 1)
                half = pl.multiple_of((block & 1) * SIDE, SIDE)
                piece = got_ref[owner, pl.ds(row, SLICE), pl.ds(half, SIDE)]
                out_ref[quad, pl.ds(row, SLICE), pl.ds(t * SIDE, SIDE)] = piece
                out_ref[quad + n // 2, pl.ds(row, SLICE), pl.ds(t * SIDE, SIDE)] = piece


def block_of(ref, row, slot):
    piece = ref[:, pl.ds(row, SLICE), pl.ds(slot * SIDE, SIDE)]
    return piece.reshape(-1, SIDE)


def dot(a, b, da, db):
    return lax.dot_general(a, b, (((da,), (db,)), ((), ())), preferred_element_type=F32)


def hidden_kernel(own_ref, oth_ref, win_ref, wout_ref, grads_ref, act_ref, dpre_ref):
    j = pl.program_id(0)
    slots = [j, j ^ 1, j ^ 2]
    xs = [block_of(own_ref, 0, s) for s in slots] + [block_of(oth_ref, 0, j)]
    dys = [block_of(own_ref, SLICE, s) for s in slots] + [block_of(oth_ref, SLICE, j)]
    pre = sum(dot(xs[k], win_ref[0, k], 1, 0) for k in range(4))
    d_act = sum(dot(dys[k], wout_ref[0, k], 1, 1) for k in range(4))
    c = math.sqrt(2.0 / math.pi)
    square = pre * pre
    th = jnp.tanh(c * (pre + 0.044715 * (square * pre)))
    half = 0.5 * (1.0 + th)
    act = (pre * half).astype(BF16)
    slope = half + (0.5 * c) * pre * (1.0 - th * th) * (1.0 + (3 * 0.044715) * square)
    d_pre = (d_act * slope).astype(BF16)
    act_ref[...] = act
    dpre_ref[...] = d_pre
    zs, xl = grads_ref.shape[0], grads_ref.shape[1]
    for k in range(4):
        g_in = dot(xs[k], d_pre, 0, 0).astype(BF16)
        g_out = dot(act, dys[k], 0, 0).astype(BF16)
        grads_ref[:, :, 0, 0, k] = g_in.reshape(zs, xl, SLICE, SIDE)
        grads_ref[:, :, 1, 0, k] = g_out.reshape(zs, xl, SLICE, SIDE)


def project_kernel(act_ref, dpre_ref, win_ref, wout_ref, own_ref, oth_ref):
    acts = [act_ref[:, t * SIDE : (t + 1) * SIDE] for t in range(4)]
    dpres = [dpre_ref[:, t * SIDE : (t + 1) * SIDE] for t in range(4)]
    for s in range(4):
        lanes = pl.ds(s * SIDE, SIDE)
        own = sum(dot(acts[s ^ m], wout_ref[s ^ m, k], 1, 0) for k, m in enumerate((0, 1, 2)))
        oth = dot(acts[s], wout_ref[s, 3], 1, 0)
        own_ref[:, :SLICE, lanes] = own.astype(BF16).reshape(-1, SLICE, SIDE)
        oth_ref[:, :SLICE, lanes] = oth.astype(BF16).reshape(-1, SLICE, SIDE)
        own = sum(dot(dpres[s ^ m], win_ref[s ^ m, k], 1, 1) for k, m in enumerate((0, 1, 2)))
        oth = dot(dpres[s], win_ref[s, 3], 1, 1)
        own_ref[:, SLICE:, lanes] = own.astype(BF16).reshape(-1, SLICE, SIDE)
        oth_ref[:, SLICE:, lanes] = oth.astype(BF16).reshape(-1, SLICE, SIDE)


def sort_kernel(n, table, got_ref, out_ref):
    for quad in range(n // 2):
        for t in range(4):
            for row, column in ((0, t + 4), (SLICE, t)):
                block = table[quad, column]
                owner = lax.shift_right_logical(block, 1)
                half = pl.multiple_of((block & 1) * SIDE, SIDE)
                rows, lanes = pl.ds(row, SLICE), pl.ds(t * SIDE, SIDE)
                total = got_ref[quad, rows, lanes].astype(F32)
                total = total + got_ref[quad + n // 2, rows, lanes].astype(F32)
                out_ref[owner, rows, pl.ds(half, SIDE)] = total.astype(BF16)


def shards(tokens, cotangent, w_in, w_out, in_blocks, out_blocks):
    n = lax.axis_size("mp")
    n_dp = lax.axis_size("dp")
    zs = n_dp // 2
    tok = tokens.shape[0]
    total_tok = tok * n_dp
    mate = [(i, i ^ 1) for i in range(n)]

    packed = pl.pallas_call(
        functools.partial(pack_kernel, n),
        out_shape=jax.ShapeDtypeStruct((n, 2 * SLICE, 2 * SIDE + 128), BF16),
        in_specs=[VMEM, VMEM, SMEM, SMEM],
        out_specs=VMEM,
        compiler_params=params(),
        name="pack",
    )(tokens, cotangent, in_blocks, out_blocks)
    got = lax.all_to_all(packed, "mp", 0, 0, tiled=True)
    chosen, table = pl.pallas_call(
        functools.partial(select_kernel, n),
        out_shape=(
            jax.ShapeDtypeStruct((n, 2 * SLICE, QUAD), BF16),
            jax.ShapeDtypeStruct((n, 128), jnp.int32),
        ),
        in_specs=[VMEM],
        out_specs=(VMEM, VMEM),
        scratch_shapes=[pltpu.SMEM((n, 128), jnp.int32), pltpu.SemaphoreType.DMA],
        compiler_params=params(),
        name="select",
    )(got)
    own = lax.all_to_all(chosen, "mp", 0, 0, tiled=True)
    oth = lax.ppermute(own, "mp", mate)

    whole = lambda shape: pl.BlockSpec(shape, lambda j: (0,) * len(shape))
    grads, act, d_pre = pl.pallas_call(
        hidden_kernel,
        grid=(4,),
        out_shape=(
            jax.ShapeDtypeStruct((zs, 2, 2, 4, 4, SLICE, SIDE), BF16),
            jax.ShapeDtypeStruct((tok, QUAD), BF16),
            jax.ShapeDtypeStruct((tok, QUAD), BF16),
        ),
        in_specs=[
            whole(own.shape),
            whole(oth.shape),
            pl.BlockSpec((1, 4, SIDE, SIDE), lambda j: (j, 0, 0, 0)),
            pl.BlockSpec((1, 4, SIDE, SIDE), lambda j: (j, 0, 0, 0)),
        ],
        out_specs=(
            pl.BlockSpec((zs, 2, 2, 1, 4, SLICE, SIDE), lambda j: (0, 0, 0, j, 0, 0, 0)),
            pl.BlockSpec((tok, SIDE), lambda j: (0, j)),
            pl.BlockSpec((tok, SIDE), lambda j: (0, j)),
        ),
        compiler_params=params(),
        name="hidden",
    )(own, oth, w_in, w_out)

    columns = [[z * 2 + xl for z in range(zs)] for xl in range(2)]
    grad_sum = lax.psum_scatter(
        grads.reshape(-1, SIDE), "dp", scatter_dimension=0, axis_index_groups=columns, tiled=True
    )

    share = jax.ShapeDtypeStruct((n, 2 * SLICE, QUAD), BF16)
    part_own, part_oth = pl.pallas_call(
        project_kernel,
        out_shape=(share, share),
        in_specs=[VMEM] * 4,
        out_specs=(VMEM, VMEM),
        compiler_params=params(),
        name="project",
    )(act, d_pre, w_in, w_out)
    part_mate = lax.ppermute(part_oth, "mp", mate)
    part = (part_own.astype(F32) + part_mate.astype(F32)).astype(BF16)
    slices = lax.all_to_all(part, "mp", 0, 0, tiled=True)
    sorted_ = pl.pallas_call(
        functools.partial(sort_kernel, n),
        out_shape=jax.ShapeDtypeStruct((n, 2 * SLICE, 2 * SIDE), BF16),
        in_specs=[SMEM, VMEM],
        out_specs=VMEM,
        compiler_params=params(),
        name="sort",
    )(table, slices)
    final = lax.all_to_all(sorted_, "mp", 0, 0, tiled=True)
    output = final[:, :SLICE].reshape(tok, 2 * SIDE)
    grad_tokens = final[:, SLICE:].reshape(tok, 2 * SIDE)

    side = lax.rem(lax.axis_index("dp"), 2)
    halves = grad_sum.reshape(2, 2, 4, 4, SLICE, SIDE)
    away = lax.dynamic_index_in_dim(halves, 1 - side, 0, keepdims=False)
    mine = lax.dynamic_index_in_dim(halves, side, 0, keepdims=False)
    came = lax.ppermute(away, "dp", [(i, i ^ 1) for i in range(n_dp)])
    scale = 1.0 / math.sqrt(total_tok)
    both = (mine.astype(F32) + came.astype(F32)) * scale
    return output, grad_tokens, both[0], both[1]


def solution(mesh):
    placed = (
        P("dp", "mp"),
        P("dp", "mp"),
        P("mp", None, None, None),
        P("mp", None, None, None),
        P("mp", None),
        P("mp", None),
    )
    return jax.shard_map(
        shards,
        mesh=mesh,
        in_specs=placed,
        out_specs=(
            P("dp", "mp"),
            P("dp", "mp"),
            P("mp", None, "dp", None),
            P("mp", None, "dp", None),
        ),
        check_vma=False,
    )
```

```python
import math

import jax
import jax.numpy as jnp
from jax import lax
from jax.experimental import pallas as pl
from jax.experimental.pallas import tpu as pltpu
from jax.sharding import PartitionSpec as P

SIDE = 256
QUAD = 4 * SIDE
SLICE = 16
VMEM = pl.BlockSpec(memory_space=pltpu.VMEM)
ANY = pl.BlockSpec(memory_space=pl.ANY)
SMEM = pl.BlockSpec(memory_space=pltpu.SMEM)
BF16 = jnp.bfloat16
F32 = jnp.float32


def params():
    return pltpu.CompilerParams(vmem_limit_bytes=40 * 1024 * 1024)


def pack_kernel(x_ref, dy_ref, p_ref, q_ref, out_ref, lists, sems):
    features = pl.ds(0, 2 * SIDE)
    copies = [
        pltpu.make_async_copy(p_ref, lists.at[0], sems.at[0]),
        pltpu.make_async_copy(q_ref, lists.at[1], sems.at[1]),
        pltpu.make_async_copy(x_ref, out_ref.at[:, pl.ds(0, SLICE), features], sems.at[2]),
        pltpu.make_async_copy(dy_ref, out_ref.at[:, pl.ds(SLICE, SLICE), features], sems.at[3]),
    ]
    for copy in copies:
        copy.start()
    row = lax.broadcasted_iota(jnp.int32, (4, 128), 0)
    lane = lax.broadcasted_iota(jnp.int32, (4, 128), 1)
    total = jnp.zeros((1, 128), F32)
    for part in range(2):
        copies[part].wait()
        column = jnp.broadcast_to(lists[part][:, 0:1], (4, 128)).astype(F32)
        total = total + jnp.sum(jnp.where(lane == row + 4 * part, column, 0.0), axis=0, keepdims=True)
    tail = out_ref.shape[:2] + (128,)
    out_ref[:, :, 2 * SIDE :] = jnp.broadcast_to(total[None], tail).astype(BF16)
    copies[2].wait()
    copies[3].wait()


def select_kernel(got_ref, out_ref, lists_ref, table, sem):
    lists = jnp.max(got_ref[:, :SLICE, 2 * SIDE :].astype(F32), axis=1).astype(jnp.int32)
    lists_ref[...] = lists
    copy = pltpu.make_async_copy(lists_ref, table, sem)
    copy.start()
    copy.wait()
    chips = out_ref.shape[0]
    for group in range(chips // 2):
        for slot in range(8):
            for row, column in ((0, slot % 4), (SLICE, slot % 4 + 4)):
                block = table[2 * group + slot // 4, column]
                owner = lax.shift_right_logical(block, 1)
                half = pl.multiple_of((block & 1) * SIDE, SIDE)
                piece = got_ref[owner, pl.ds(row, SLICE), pl.ds(half, SIDE)]
                out_ref[group, slot, pl.ds(row, SLICE), :] = piece
                out_ref[group + chips // 2, slot, pl.ds(row, SLICE), :] = piece


def dot(a, b, da, db):
    return lax.dot_general(a, b, (((da,), (db,)), ((), ())), preferred_element_type=F32)


def slots_of(j):
    core = lax.axis_index("mp") & 1
    return [4 * core + (j ^ m) for m in (0, 1, 2)] + [4 * (1 - core) + j]


def hidden_kernel(own_ref, oth_ref, win_ref, wout_ref, grads_ref, act_ref, dpre_ref, held, sems):
    def block_of(row, slot):
        pieces = [ref[:, slot, pl.ds(row, SLICE), :].reshape(-1, SIDE) for ref in (own_ref, oth_ref)]
        return jnp.concatenate(pieces, axis=0)

    side = lax.axis_index("dp") & 1
    c = math.sqrt(2.0 / math.pi)
    copies = []
    for j in range(4):
        slots = slots_of(j)
        xs = [block_of(0, s) for s in slots]
        dys = [block_of(SLICE, s) for s in slots]
        pre = sum(dot(xs[k], win_ref[j, k], 1, 0) for k in range(4))
        d_act = sum(dot(dys[k], wout_ref[j, k], 1, 1) for k in range(4))
        square = pre * pre
        th = jnp.tanh(c * (pre + 0.044715 * (square * pre)))
        half = 0.5 * (1.0 + th)
        act = (pre * half).astype(BF16)
        slope = half + (0.5 * c) * pre * (1.0 - th * th) * (1.0 + (3 * 0.044715) * square)
        d_pre = (d_act * slope).astype(BF16)
        act_ref[:, j * SIDE : (j + 1) * SIDE] = act
        dpre_ref[:, j * SIDE : (j + 1) * SIDE] = d_pre
        zs = held.shape[1]
        for k in range(4):
            g_in = dot(xs[k], d_pre, 0, 0).astype(BF16).reshape(zs, 2, SLICE, SIDE)
            g_out = dot(act, dys[k], 0, 0).astype(BF16).reshape(zs, 2, SLICE, SIDE)
            for away in range(2):
                held[j, :, away ^ side, 0, k] = g_in[:, away]
                held[j, :, away ^ side, 1, k] = g_out[:, away]
        copies.append(pltpu.make_async_copy(held.at[j], grads_ref.at[:, :, :, j], sems.at[j]))
        copies[-1].start()
    for copy in copies:
        copy.wait()


def project_kernel(act_ref, dpre_ref, win_ref, wout_ref, own_ref, oth_ref):
    core = lax.axis_index("mp") & 1
    acts = [act_ref[:, t * SIDE : (t + 1) * SIDE] for t in range(4)]
    dpres = [dpre_ref[:, t * SIDE : (t + 1) * SIDE] for t in range(4)]

    def put(row, slot, total):
        pieces = total.astype(BF16).reshape(2, -1, SLICE, SIDE)
        own_ref[:, slot, pl.ds(row, SLICE), :] = pieces[0]
        oth_ref[:, slot, pl.ds(row, SLICE), :] = pieces[1]

    for s in range(4):
        near, far = 4 * core + s, 4 * (1 - core) + s
        three = [(k, s ^ m) for k, m in enumerate((0, 1, 2))]
        put(0, near, sum(dot(acts[j], wout_ref[j, k], 1, 0) for k, j in three))
        put(0, far, dot(acts[s], wout_ref[s, 3], 1, 0))
        put(SLICE, near, sum(dot(dpres[j], win_ref[j, k], 1, 1) for k, j in three))
        put(SLICE, far, dot(dpres[s], win_ref[s, 3], 1, 1))


def sort_kernel(table, got_ref, out_ref):
    chips = got_ref.shape[0]
    for group in range(chips // 2):
        for slot in range(8):
            for row, column in ((0, slot % 4 + 4), (SLICE, slot % 4)):
                block = table[2 * group + slot // 4, column]
                owner = lax.shift_right_logical(block, 1)
                half = pl.multiple_of((block & 1) * SIDE, SIDE)
                rows = pl.ds(row, SLICE)
                total = got_ref[group, slot, rows, :].astype(F32)
                total = total + got_ref[group + chips // 2, slot, rows, :].astype(F32)
                out_ref[owner, rows, pl.ds(half, SIDE)] = total.astype(BF16)


def shards(tokens, cotangent, w_in, w_out, in_blocks, out_blocks):
    n = lax.axis_size("mp")
    n_dp = lax.axis_size("dp")
    zs = n_dp // 2
    tok = tokens.shape[0]
    total_tok = tok * n_dp
    mate = [(i, i ^ 1) for i in range(n)]
    same_core = [[2 * chip + core for chip in range(n // 2)] for core in range(2)]

    packed = pl.pallas_call(
        pack_kernel,
        out_shape=jax.ShapeDtypeStruct((n, 2 * SLICE, 2 * SIDE + 128), BF16),
        in_specs=[ANY] * 4,
        out_specs=VMEM,
        scratch_shapes=[pltpu.VMEM((2, 4, 4), jnp.int32), pltpu.SemaphoreType.DMA((4,))],
        compiler_params=params(),
        name="pack",
    )(
        tokens.reshape(n, SLICE, 2 * SIDE),
        cotangent.reshape(n, SLICE, 2 * SIDE),
        in_blocks,
        out_blocks,
    )
    got = lax.all_to_all(packed, "mp", 0, 0, tiled=True)
    share = jax.ShapeDtypeStruct((n // 2, 8, 2 * SLICE, SIDE), BF16)
    chosen, table = pl.pallas_call(
        select_kernel,
        out_shape=(share, jax.ShapeDtypeStruct((n, 128), jnp.int32)),
        in_specs=[VMEM],
        out_specs=(VMEM, VMEM),
        scratch_shapes=[pltpu.SMEM((n, 128), jnp.int32), pltpu.SemaphoreType.DMA],
        compiler_params=params(),
        name="select",
    )(got)
    own = lax.all_to_all(chosen, "mp", 0, 0, axis_index_groups=same_core, tiled=True)
    oth = lax.ppermute(own, "mp", mate)

    quad = jax.ShapeDtypeStruct((tok, QUAD), BF16)
    grads, act, d_pre = pl.pallas_call(
        hidden_kernel,
        out_shape=(jax.ShapeDtypeStruct((zs, 2, 2, 4, 4, SLICE, SIDE), BF16), quad, quad),
        in_specs=[VMEM] * 4,
        out_specs=(ANY, VMEM, VMEM),
        scratch_shapes=[
            pltpu.VMEM((4, zs, 2, 2, 4, SLICE, SIDE), BF16),
            pltpu.SemaphoreType.DMA((4,)),
        ],
        compiler_params=params(),
        name="hidden",
    )(own, oth, w_in, w_out)

    columns = [[z * 2 + xl for z in range(zs)] for xl in range(2)]
    grad_sum = lax.psum_scatter(
        grads.reshape(-1, SIDE), "dp", scatter_dimension=0, axis_index_groups=columns, tiled=True
    )

    part_own, part_oth = pl.pallas_call(
        project_kernel,
        out_shape=(share, share),
        in_specs=[VMEM] * 4,
        out_specs=(VMEM, VMEM),
        compiler_params=params(),
        name="project",
    )(act, d_pre, w_in, w_out)
    part_mate = lax.ppermute(part_oth, "mp", mate)
    part = (part_own.astype(F32) + part_mate.astype(F32)).astype(BF16)
    slices = lax.all_to_all(part, "mp", 0, 0, axis_index_groups=same_core, tiled=True)
    sorted_ = pl.pallas_call(
        sort_kernel,
        out_shape=jax.ShapeDtypeStruct((n, 2 * SLICE, 2 * SIDE), BF16),
        in_specs=[SMEM, VMEM],
        out_specs=VMEM,
        compiler_params=params(),
        name="sort",
    )(table, slices)
    final = lax.all_to_all(sorted_, "mp", 0, 0, tiled=True)
    output = final[:, :SLICE].reshape(tok, 2 * SIDE)
    grad_tokens = final[:, SLICE:].reshape(tok, 2 * SIDE)

    grad_sum, output, grad_tokens = lax.optimization_barrier((grad_sum, output, grad_tokens))
    halves = grad_sum.reshape(2, 2, 4, 4, SLICE, SIDE)
    came = lax.ppermute(halves[1], "dp", [(i, i ^ 1) for i in range(n_dp)])
    scale = 1.0 / math.sqrt(total_tok)
    both = (halves[0].astype(F32) + came.astype(F32)) * scale
    return output, grad_tokens, both[0], both[1]


def solution(mesh):
    placed = (
        P("dp", "mp"),
        P("dp", "mp"),
        P("mp", None, None, None),
        P("mp", None, None, None),
        P("mp", None),
        P("mp", None),
    )
    return jax.shard_map(
        shards,
        mesh=mesh,
        in_specs=placed,
        out_specs=(
            P("dp", "mp"),
            P("dp", "mp"),
            P("mp", None, "dp", None),
            P("mp", None, "dp", None),
        ),
        check_vma=False,
    )
```

```python
import functools
import math

import jax
import jax.numpy as jnp
from jax import lax
from jax.experimental import pallas as pl
from jax.experimental.pallas import tpu as pltpu
from jax.sharding import PartitionSpec as P

SIDE = 256
QUAD = 4 * SIDE
SLICE = 16
LANES = 128
TILES = 2 * SIDE // LANES
VMEM = pl.BlockSpec(memory_space=pltpu.VMEM)
HBM = pl.BlockSpec(memory_space=pltpu.HBM)
SMEM = pl.BlockSpec(memory_space=pltpu.SMEM)
BF16 = jnp.bfloat16
F32 = jnp.float32


def in_hbm(array):
    return pltpu.with_memory_space_constraint(array, pltpu.HBM)


def params():
    return pltpu.CompilerParams(vmem_limit_bytes=40 * 1024 * 1024)


def pack_kernel(x_ref, dy_ref, p_ref, q_ref, out_ref, lists, sems):
    copies = [
        pltpu.make_async_copy(p_ref, lists.at[0], sems.at[0]),
        pltpu.make_async_copy(q_ref, lists.at[1], sems.at[1]),
    ]
    for part, ref in enumerate((x_ref, dy_ref)):
        for tile in range(TILES):
            at = part * TILES + tile
            source = ref.at[:, :, pl.ds(tile * LANES, LANES)]
            target = out_ref.at[:, pl.ds(at * SLICE, SLICE), :]
            copies.append(pltpu.make_async_copy(source, target, sems.at[2 + at]))
    for copy in copies:
        copy.start()
    row = lax.broadcasted_iota(jnp.int32, (4, LANES), 0)
    lane = lax.broadcasted_iota(jnp.int32, (4, LANES), 1)
    total = jnp.zeros((1, LANES), F32)
    for part in range(2):
        copies[part].wait()
        column = jnp.broadcast_to(lists[part][:, 0:1], (4, LANES)).astype(F32)
        total = total + jnp.sum(jnp.where(lane == row + 4 * part, column, 0.0), axis=0, keepdims=True)
    shape = (out_ref.shape[0], SLICE, LANES)
    out_ref[:, pl.ds(2 * TILES * SLICE, SLICE), :] = jnp.broadcast_to(total[None], shape).astype(BF16)
    for copy in copies[2:]:
        copy.wait()


def select_kernel(got_ref, out_ref, lists_ref, table, sem):
    lists = jnp.max(got_ref[:, pl.ds(2 * TILES * SLICE, SLICE), :].astype(F32), axis=1).astype(jnp.int32)
    lists_ref[...] = lists
    copy = pltpu.make_async_copy(lists_ref, table, sem)
    copy.start()
    copy.wait()
    chips = out_ref.shape[0]
    for group in range(chips // 2):
        for slot in range(8):
            for row, column in ((0, slot % 4), (SLICE, slot % 4 + 4)):
                block = table[2 * group + slot // 4, column]
                owner = lax.shift_right_logical(block, 1)
                first = row * TILES + (block & 1) * (2 * SLICE)
                for tile in range(2):
                    rows = pl.ds(pl.multiple_of(first + tile * SLICE, SLICE), SLICE)
                    piece = got_ref[owner, rows, :]
                    lanes = pl.ds(tile * LANES, LANES)
                    out_ref[group, slot, pl.ds(row, SLICE), lanes] = piece
                    out_ref[group + chips // 2, slot, pl.ds(row, SLICE), lanes] = piece


def dot(a, b, da, db):
    return lax.dot_general(a, b, (((da,), (db,)), ((), ())), preferred_element_type=F32)


def slots_of(j):
    core = lax.axis_index("mp") & 1
    return [4 * core + (j ^ m) for m in (0, 1, 2)] + [4 * (1 - core) + j]


def hidden_kernel(own_ref, oth_ref, win_ref, wout_ref, grads_ref, act_ref, dpre_ref, held, sems):
    def block_of(row, slot):
        pieces = [ref[:, slot, pl.ds(row, SLICE), :].reshape(-1, SIDE) for ref in (own_ref, oth_ref)]
        return jnp.concatenate(pieces, axis=0)

    side = lax.axis_index("dp") & 1
    c = math.sqrt(2.0 / math.pi)
    copies = []
    for j in range(4):
        slots = slots_of(j)
        xs = [block_of(0, s) for s in slots]
        dys = [block_of(SLICE, s) for s in slots]
        pre = sum(dot(xs[k], win_ref[j, k], 1, 0) for k in range(4))
        d_act = sum(dot(dys[k], wout_ref[j, k], 1, 1) for k in range(4))
        square = pre * pre
        th = jnp.tanh(c * (pre + 0.044715 * (square * pre)))
        half = 0.5 * (1.0 + th)
        act = (pre * half).astype(BF16)
        slope = half + (0.5 * c) * pre * (1.0 - th * th) * (1.0 + (3 * 0.044715) * square)
        d_pre = (d_act * slope).astype(BF16)
        act_ref[:, j * SIDE : (j + 1) * SIDE] = act
        dpre_ref[:, j * SIDE : (j + 1) * SIDE] = d_pre
        zs = held.shape[1]
        for k in range(4):
            g_in = dot(xs[k], d_pre, 0, 0).astype(BF16).reshape(zs, 2, SLICE, SIDE)
            g_out = dot(act, dys[k], 0, 0).astype(BF16).reshape(zs, 2, SLICE, SIDE)
            for away in range(2):
                held[j, :, away ^ side, 0, k] = g_in[:, away]
                held[j, :, away ^ side, 1, k] = g_out[:, away]
        copies.append(pltpu.make_async_copy(held.at[j], grads_ref.at[:, :, :, j], sems.at[j]))
        copies[-1].start()
    for copy in copies:
        copy.wait()


def project_kernel(act_ref, dpre_ref, win_ref, wout_ref, own_ref, oth_ref):
    core = lax.axis_index("mp") & 1
    acts = [act_ref[:, t * SIDE : (t + 1) * SIDE] for t in range(4)]
    dpres = [dpre_ref[:, t * SIDE : (t + 1) * SIDE] for t in range(4)]

    def put(row, slot, total):
        pieces = total.astype(BF16).reshape(2, -1, SLICE, SIDE)
        own_ref[:, slot, pl.ds(row, SLICE), :] = pieces[0]
        oth_ref[:, slot, pl.ds(row, SLICE), :] = pieces[1]

    for s in range(4):
        near, far = 4 * core + s, 4 * (1 - core) + s
        three = [(k, s ^ m) for k, m in enumerate((0, 1, 2))]
        put(0, near, sum(dot(acts[j], wout_ref[j, k], 1, 0) for k, j in three))
        put(0, far, dot(acts[s], wout_ref[s, 3], 1, 0))
        put(SLICE, near, sum(dot(dpres[j], win_ref[j, k], 1, 1) for k, j in three))
        put(SLICE, far, dot(dpres[s], win_ref[s, 3], 1, 1))


def sort_kernel(table, got_ref, out_ref):
    chips = got_ref.shape[0]
    for group in range(chips // 2):
        for slot in range(8):
            for row, column in ((0, slot % 4 + 4), (SLICE, slot % 4)):
                block = table[2 * group + slot // 4, column]
                owner = lax.shift_right_logical(block, 1)
                half = pl.multiple_of((block & 1) * SIDE, SIDE)
                rows = pl.ds(row, SLICE)
                total = got_ref[group, slot, rows, :].astype(F32)
                total = total + got_ref[group + chips // 2, slot, rows, :].astype(F32)
                out_ref[owner, rows, pl.ds(half, SIDE)] = total.astype(BF16)


def finish_kernel(scale, own_ref, came_ref, in_ref, out_ref):
    for which, ref in enumerate((in_ref, out_ref)):
        ref[...] = (own_ref[0, which].astype(F32) + came_ref[which].astype(F32)) * scale


def shards(tokens, cotangent, w_in, w_out, in_blocks, out_blocks):
    n = lax.axis_size("mp")
    n_dp = lax.axis_size("dp")
    zs = n_dp // 2
    tok = tokens.shape[0]
    total_tok = tok * n_dp
    mate = [(i, i ^ 1) for i in range(n)]
    same_core = [[2 * chip + core for chip in range(n // 2)] for core in range(2)]

    packed = pl.pallas_call(
        pack_kernel,
        out_shape=jax.ShapeDtypeStruct((n, (2 * TILES + 1) * SLICE, LANES), BF16),
        in_specs=[HBM] * 4,
        out_specs=VMEM,
        scratch_shapes=[pltpu.VMEM((2, 4, 4), jnp.int32), pltpu.SemaphoreType.DMA((2 + 2 * TILES,))],
        compiler_params=params(),
        name="pack",
    )(
        in_hbm(tokens.reshape(n, SLICE, 2 * SIDE)),
        in_hbm(cotangent.reshape(n, SLICE, 2 * SIDE)),
        in_hbm(in_blocks),
        in_hbm(out_blocks),
    )
    got = lax.all_to_all(packed, "mp", 0, 0, tiled=True)
    share = jax.ShapeDtypeStruct((n // 2, 8, 2 * SLICE, SIDE), BF16)
    chosen, table = pl.pallas_call(
        select_kernel,
        out_shape=(share, jax.ShapeDtypeStruct((n, LANES), jnp.int32)),
        in_specs=[VMEM],
        out_specs=(VMEM, VMEM),
        scratch_shapes=[pltpu.SMEM((n, LANES), jnp.int32), pltpu.SemaphoreType.DMA],
        compiler_params=params(),
        name="select",
    )(got)
    own = lax.all_to_all(chosen, "mp", 0, 0, axis_index_groups=same_core, tiled=True)
    oth = lax.ppermute(own, "mp", mate)

    quad = jax.ShapeDtypeStruct((tok, QUAD), BF16)
    grads, act, d_pre = pl.pallas_call(
        hidden_kernel,
        out_shape=(pltpu.HBM((zs, 2, 2, 4, 4, SLICE, SIDE), BF16), quad, quad),
        in_specs=[VMEM] * 4,
        out_specs=(HBM, VMEM, VMEM),
        scratch_shapes=[
            pltpu.VMEM((4, zs, 2, 2, 4, SLICE, SIDE), BF16),
            pltpu.SemaphoreType.DMA((4,)),
        ],
        compiler_params=params(),
        name="hidden",
    )(own, oth, w_in, w_out)

    columns = [[z * 2 + xl for z in range(zs)] for xl in range(2)]
    grad_sum = lax.psum_scatter(
        grads.reshape(-1, SIDE), "dp", scatter_dimension=0, axis_index_groups=columns, tiled=True
    )

    part_own, part_oth = pl.pallas_call(
        project_kernel,
        out_shape=(share, share),
        in_specs=[VMEM] * 4,
        out_specs=(VMEM, VMEM),
        compiler_params=params(),
        name="project",
    )(act, d_pre, w_in, w_out)
    part_mate = lax.ppermute(part_oth, "mp", mate)
    part = (part_own.astype(F32) + part_mate.astype(F32)).astype(BF16)
    slices = lax.all_to_all(part, "mp", 0, 0, axis_index_groups=same_core, tiled=True)
    sorted_ = pl.pallas_call(
        sort_kernel,
        out_shape=jax.ShapeDtypeStruct((n, 2 * SLICE, 2 * SIDE), BF16),
        in_specs=[SMEM, VMEM],
        out_specs=VMEM,
        compiler_params=params(),
        name="sort",
    )(table, slices)
    final = lax.all_to_all(sorted_, "mp", 0, 0, tiled=True)
    output = final[:, :SLICE].reshape(tok, 2 * SIDE)
    grad_tokens = final[:, SLICE:].reshape(tok, 2 * SIDE)

    grad_sum, output, grad_tokens = lax.optimization_barrier((grad_sum, output, grad_tokens))
    halves = grad_sum.reshape(2, 2, 4, 4, SLICE, SIDE)
    came = lax.ppermute(halves[1], "dp", [(i, i ^ 1) for i in range(n_dp)])
    grad_shape = jax.ShapeDtypeStruct((4, 4, SLICE, SIDE), F32)
    grad_in, grad_out = pl.pallas_call(
        functools.partial(finish_kernel, 1.0 / math.sqrt(total_tok)),
        grid=(1,),
        out_shape=(grad_shape, grad_shape),
        in_specs=[
            pl.BlockSpec((1, 2, 4, 4, SLICE, SIDE), lambda i: (0,) * 6),
            pl.BlockSpec((2, 4, 4, SLICE, SIDE), lambda i: (0,) * 5),
        ],
        out_specs=(
            pl.BlockSpec((4, 4, SLICE, SIDE), lambda i: (0,) * 4),
            pl.BlockSpec((4, 4, SLICE, SIDE), lambda i: (0,) * 4),
        ),
        compiler_params=params(),
        name="finish",
    )(in_hbm(halves), came)
    return output, grad_tokens, grad_in, grad_out


def solution(mesh):
    placed = (
        P("dp", "mp"),
        P("dp", "mp"),
        P("mp", None, None, None),
        P("mp", None, None, None),
        P("mp", None),
        P("mp", None),
    )
    return jax.shard_map(
        shards,
        mesh=mesh,
        in_specs=placed,
        out_specs=(
            P("dp", "mp"),
            P("dp", "mp"),
            P("mp", None, "dp", None),
            P("mp", None, "dp", None),
        ),
        check_vma=False,
    )
```

```python
import functools
import math

import jax
import jax.numpy as jnp
from jax import lax
from jax.experimental import pallas as pl
from jax.experimental.pallas import tpu as pltpu
from jax.sharding import PartitionSpec as P

SIDE = 256
QUAD = 4 * SIDE
SLICE = 16
LANES = 128
TILES = 2 * SIDE // LANES
VMEM = pl.BlockSpec(memory_space=pltpu.VMEM)
HBM = pl.BlockSpec(memory_space=pltpu.HBM)
SMEM = pl.BlockSpec(memory_space=pltpu.SMEM)
BF16 = jnp.bfloat16
F32 = jnp.float32


def in_hbm(array):
    return pltpu.with_memory_space_constraint(array, pltpu.HBM)


def params():
    return pltpu.CompilerParams(vmem_limit_bytes=40 * 1024 * 1024)


def pack_kernel(x_ref, dy_ref, p_ref, q_ref, out_ref, lists, sems):
    copies = [
        pltpu.make_async_copy(p_ref, lists.at[0], sems.at[0]),
        pltpu.make_async_copy(q_ref, lists.at[1], sems.at[1]),
    ]
    for part, ref in enumerate((x_ref, dy_ref)):
        for tile in range(TILES):
            at = part * TILES + tile
            source = ref.at[:, :, pl.ds(tile * LANES, LANES)]
            target = out_ref.at[:, pl.ds(at * SLICE, SLICE), :]
            copies.append(pltpu.make_async_copy(source, target, sems.at[2 + at]))
    for copy in copies:
        copy.start()
    row = lax.broadcasted_iota(jnp.int32, (4, LANES), 0)
    lane = lax.broadcasted_iota(jnp.int32, (4, LANES), 1)
    total = jnp.zeros((1, LANES), F32)
    for part in range(2):
        copies[part].wait()
        column = jnp.broadcast_to(lists[part][:, 0:1], (4, LANES)).astype(F32)
        total = total + jnp.sum(jnp.where(lane == row + 4 * part, column, 0.0), axis=0, keepdims=True)
    shape = (out_ref.shape[0], SLICE, LANES)
    out_ref[:, pl.ds(2 * TILES * SLICE, SLICE), :] = jnp.broadcast_to(total[None], shape).astype(BF16)
    for copy in copies[2:]:
        copy.wait()


def select_kernel(got_ref, out_ref, lists_ref, table, sem):
    lists = jnp.max(got_ref[:, pl.ds(2 * TILES * SLICE, SLICE), :].astype(F32), axis=1).astype(jnp.int32)
    lists_ref[...] = lists
    copy = pltpu.make_async_copy(lists_ref, table, sem)
    copy.start()
    copy.wait()
    chips = out_ref.shape[0]
    for group in range(chips // 2):
        for slot in range(8):
            for row, column in ((0, slot % 4), (SLICE, slot % 4 + 4)):
                block = table[2 * group + slot // 4, column]
                owner = lax.shift_right_logical(block, 1)
                first = row * TILES + (block & 1) * (2 * SLICE)
                for tile in range(2):
                    rows = pl.ds(pl.multiple_of(first + tile * SLICE, SLICE), SLICE)
                    piece = got_ref[owner, rows, :]
                    lanes = pl.ds(tile * LANES, LANES)
                    out_ref[group, slot, pl.ds(row, SLICE), lanes] = piece
                    out_ref[group + chips // 2, slot, pl.ds(row, SLICE), lanes] = piece


def dot(a, b, da, db):
    return lax.dot_general(a, b, (((da,), (db,)), ((), ())), preferred_element_type=F32)


def slots_of(j):
    core = lax.axis_index("mp") & 1
    return [4 * core + (j ^ m) for m in (0, 1, 2)] + [4 * (1 - core) + j]


def hidden_kernel(own_ref, oth_ref, win_ref, wout_ref, grads_ref, act_ref, dpre_ref, held, sems):
    def block_of(row, slot):
        pieces = [ref[:, slot, pl.ds(row, SLICE), :].reshape(-1, SIDE) for ref in (own_ref, oth_ref)]
        return jnp.concatenate(pieces, axis=0)

    side = lax.axis_index("dp") & 1
    c = math.sqrt(2.0 / math.pi)
    copies = []
    for j in range(4):
        slots = slots_of(j)
        xs = [block_of(0, s) for s in slots]
        dys = [block_of(SLICE, s) for s in slots]
        pre = sum(dot(xs[k], win_ref[j, k], 1, 0) for k in range(4))
        d_act = sum(dot(dys[k], wout_ref[j, k], 1, 1) for k in range(4))
        square = pre * pre
        th = jnp.tanh(c * (pre + 0.044715 * (square * pre)))
        half = 0.5 * (1.0 + th)
        act = (pre * half).astype(BF16)
        slope = half + (0.5 * c) * pre * (1.0 - th * th) * (1.0 + (3 * 0.044715) * square)
        d_pre = (d_act * slope).astype(BF16)
        act_ref[:, j * SIDE : (j + 1) * SIDE] = act
        dpre_ref[:, j * SIDE : (j + 1) * SIDE] = d_pre
        zs = held.shape[2]
        for k in range(4):
            g_in = dot(xs[k], d_pre, 0, 0).astype(BF16).reshape(zs, 2, SLICE, SIDE)
            g_out = dot(act, dys[k], 0, 0).astype(BF16).reshape(zs, 2, SLICE, SIDE)
            for away in range(2):
                held[j, k, :, away ^ side, 0] = g_in[:, away]
                held[j, k, :, away ^ side, 1] = g_out[:, away]
            copies.append(pltpu.make_async_copy(held.at[j, k], grads_ref.at[:, :, :, j, k], sems.at[j, k]))
            copies[-1].start()
    for copy in copies:
        copy.wait()


def project_kernel(act_ref, dpre_ref, win_ref, wout_ref, own_ref, oth_ref):
    core = lax.axis_index("mp") & 1
    acts = [act_ref[:, t * SIDE : (t + 1) * SIDE] for t in range(4)]
    dpres = [dpre_ref[:, t * SIDE : (t + 1) * SIDE] for t in range(4)]

    def put(row, slot, total):
        pieces = total.astype(BF16).reshape(2, -1, SLICE, SIDE)
        own_ref[:, slot, pl.ds(row, SLICE), :] = pieces[0]
        oth_ref[:, slot, pl.ds(row, SLICE), :] = pieces[1]

    for s in range(4):
        near, far = 4 * core + s, 4 * (1 - core) + s
        three = [(k, s ^ m) for k, m in enumerate((0, 1, 2))]
        put(0, near, sum(dot(acts[j], wout_ref[j, k], 1, 0) for k, j in three))
        put(0, far, dot(acts[s], wout_ref[s, 3], 1, 0))
        put(SLICE, near, sum(dot(dpres[j], win_ref[j, k], 1, 1) for k, j in three))
        put(SLICE, far, dot(dpres[s], win_ref[s, 3], 1, 1))


def sort_kernel(table, got_ref, out_ref):
    chips = got_ref.shape[0]
    for group in range(chips // 2):
        for slot in range(8):
            for row, column in ((0, slot % 4 + 4), (SLICE, slot % 4)):
                block = table[2 * group + slot // 4, column]
                owner = lax.shift_right_logical(block, 1)
                half = pl.multiple_of((block & 1) * SIDE, SIDE)
                rows = pl.ds(row, SLICE)
                total = got_ref[group, slot, rows, :].astype(F32)
                total = total + got_ref[group + chips // 2, slot, rows, :].astype(F32)
                out_ref[owner, rows, pl.ds(half, SIDE)] = total.astype(BF16)


def fetch_kernel(sum_ref, own_ref, away_ref, sems):
    copies = [
        pltpu.make_async_copy(sum_ref.at[half], ref, sems.at[half])
        for half, ref in enumerate((own_ref, away_ref))
    ]
    for copy in copies:
        copy.start()
    for copy in copies:
        copy.wait()


def finish_kernel(scale, own_ref, came_ref, in_ref, out_ref, held, sems):
    copies = []
    for which, ref in enumerate((in_ref, out_ref)):
        held[which] = (own_ref[which].astype(F32) + came_ref[which].astype(F32)) * scale
        copies.append(pltpu.make_async_copy(held.at[which], ref, sems.at[which]))
        copies[-1].start()
    for copy in copies:
        copy.wait()


def shards(tokens, cotangent, w_in, w_out, in_blocks, out_blocks):
    n = lax.axis_size("mp")
    n_dp = lax.axis_size("dp")
    zs = n_dp // 2
    tok = tokens.shape[0]
    total_tok = tok * n_dp
    mate = [(i, i ^ 1) for i in range(n)]
    same_core = [[2 * chip + core for chip in range(n // 2)] for core in range(2)]

    packed = pl.pallas_call(
        pack_kernel,
        out_shape=jax.ShapeDtypeStruct((n, (2 * TILES + 1) * SLICE, LANES), BF16),
        in_specs=[HBM] * 4,
        out_specs=VMEM,
        scratch_shapes=[pltpu.VMEM((2, 4, 4), jnp.int32), pltpu.SemaphoreType.DMA((2 + 2 * TILES,))],
        compiler_params=params(),
        name="pack",
    )(
        in_hbm(tokens.reshape(n, SLICE, 2 * SIDE)),
        in_hbm(cotangent.reshape(n, SLICE, 2 * SIDE)),
        in_hbm(in_blocks),
        in_hbm(out_blocks),
    )
    got = lax.all_to_all(packed, "mp", 0, 0, tiled=True)
    share = jax.ShapeDtypeStruct((n // 2, 8, 2 * SLICE, SIDE), BF16)
    chosen, table = pl.pallas_call(
        select_kernel,
        out_shape=(share, jax.ShapeDtypeStruct((n, LANES), jnp.int32)),
        in_specs=[VMEM],
        out_specs=(VMEM, VMEM),
        scratch_shapes=[pltpu.SMEM((n, LANES), jnp.int32), pltpu.SemaphoreType.DMA],
        compiler_params=params(),
        name="select",
    )(got)
    own = lax.all_to_all(chosen, "mp", 0, 0, axis_index_groups=same_core, tiled=True)
    oth = lax.ppermute(own, "mp", mate)

    quad = jax.ShapeDtypeStruct((tok, QUAD), BF16)
    grads, act, d_pre = pl.pallas_call(
        hidden_kernel,
        out_shape=(pltpu.HBM((zs, 2, 2, 4, 4, SLICE, SIDE), BF16), quad, quad),
        in_specs=[VMEM] * 4,
        out_specs=(HBM, VMEM, VMEM),
        scratch_shapes=[
            pltpu.VMEM((4, 4, zs, 2, 2, SLICE, SIDE), BF16),
            pltpu.SemaphoreType.DMA((4, 4)),
        ],
        compiler_params=params(),
        name="hidden",
    )(own, oth, w_in, w_out)

    columns = [[z * 2 + xl for z in range(zs)] for xl in range(2)]
    grad_sum = lax.psum_scatter(
        grads.reshape(-1, SIDE), "dp", scatter_dimension=0, axis_index_groups=columns, tiled=True
    )

    part_own, part_oth = pl.pallas_call(
        project_kernel,
        out_shape=(share, share),
        in_specs=[VMEM] * 4,
        out_specs=(VMEM, VMEM),
        compiler_params=params(),
        name="project",
    )(act, d_pre, w_in, w_out)
    part_mate = lax.ppermute(part_oth, "mp", mate)
    part = (part_own.astype(F32) + part_mate.astype(F32)).astype(BF16)
    slices = lax.all_to_all(part, "mp", 0, 0, axis_index_groups=same_core, tiled=True)
    sorted_ = pl.pallas_call(
        sort_kernel,
        out_shape=jax.ShapeDtypeStruct((n, 2 * SLICE, 2 * SIDE), BF16),
        in_specs=[SMEM, VMEM],
        out_specs=VMEM,
        compiler_params=params(),
        name="sort",
    )(table, slices)
    final = lax.all_to_all(sorted_, "mp", 0, 0, tiled=True)
    output = final[:, :SLICE].reshape(tok, 2 * SIDE)
    grad_tokens = final[:, SLICE:].reshape(tok, 2 * SIDE)

    grad_sum, output, grad_tokens = lax.optimization_barrier((grad_sum, output, grad_tokens))
    halves = grad_sum.reshape(2, 2, 4, 4, SLICE, SIDE)
    half = jax.ShapeDtypeStruct((2, 4, 4, SLICE, SIDE), BF16)
    mine, away = pl.pallas_call(
        fetch_kernel,
        out_shape=(half, half),
        in_specs=[HBM],
        out_specs=(VMEM, VMEM),
        scratch_shapes=[pltpu.SemaphoreType.DMA((2,))],
        compiler_params=params(),
        name="fetch",
    )(in_hbm(halves))
    came = lax.ppermute(away, "dp", [(i, i ^ 1) for i in range(n_dp)])
    grad_shape = pltpu.HBM((4, 4, SLICE, SIDE), F32)
    grad_in, grad_out = pl.pallas_call(
        functools.partial(finish_kernel, 1.0 / math.sqrt(total_tok)),
        out_shape=(grad_shape, grad_shape),
        in_specs=[VMEM, VMEM],
        out_specs=(HBM, HBM),
        scratch_shapes=[
            pltpu.VMEM((2, 4, 4, SLICE, SIDE), F32),
            pltpu.SemaphoreType.DMA((2,)),
        ],
        compiler_params=params(),
        name="finish",
    )(mine, came)
    return output, grad_tokens, grad_in, grad_out


def solution(mesh):
    placed = (
        P("dp", "mp"),
        P("dp", "mp"),
        P("mp", None, None, None),
        P("mp", None, None, None),
        P("mp", None),
        P("mp", None),
    )
    return jax.shard_map(
        shards,
        mesh=mesh,
        in_specs=placed,
        out_specs=(
            P("dp", "mp"),
            P("dp", "mp"),
            P("mp", None, "dp", None),
            P("mp", None, "dp", None),
        ),
        check_vma=False,
    )
```

```python
import functools
import math

import jax
import jax.numpy as jnp
from jax import lax
from jax.experimental import pallas as pl
from jax.experimental.pallas import tpu as pltpu
from jax.sharding import PartitionSpec as P

SIDE = 256
QUAD = 4 * SIDE
SLICE = 16
LANES = 128
TILES = 2 * SIDE // LANES
VMEM = pl.BlockSpec(memory_space=pltpu.VMEM)
HBM = pl.BlockSpec(memory_space=pltpu.HBM)
SMEM = pl.BlockSpec(memory_space=pltpu.SMEM)
BF16 = jnp.bfloat16
F32 = jnp.float32


def in_hbm(array):
    return pltpu.with_memory_space_constraint(array, pltpu.HBM)


def params():
    return pltpu.CompilerParams(vmem_limit_bytes=40 * 1024 * 1024)


def pack_kernel(x_ref, dy_ref, p_ref, q_ref, out_ref, lists, sems):
    copies = [
        pltpu.make_async_copy(p_ref, lists.at[0], sems.at[0]),
        pltpu.make_async_copy(q_ref, lists.at[1], sems.at[1]),
    ]
    for part, ref in enumerate((x_ref, dy_ref)):
        for tile in range(TILES):
            at = part * TILES + tile
            source = ref.at[:, :, pl.ds(tile * LANES, LANES)]
            target = out_ref.at[:, pl.ds(at * SLICE, SLICE), :]
            copies.append(pltpu.make_async_copy(source, target, sems.at[2 + at]))
    for copy in copies:
        copy.start()
    row = lax.broadcasted_iota(jnp.int32, (4, LANES), 0)
    lane = lax.broadcasted_iota(jnp.int32, (4, LANES), 1)
    total = jnp.zeros((1, LANES), F32)
    for part in range(2):
        copies[part].wait()
        column = jnp.broadcast_to(lists[part][:, 0:1], (4, LANES)).astype(F32)
        total = total + jnp.sum(jnp.where(lane == row + 4 * part, column, 0.0), axis=0, keepdims=True)
    shape = (out_ref.shape[0], SLICE, LANES)
    out_ref[:, pl.ds(2 * TILES * SLICE, SLICE), :] = jnp.broadcast_to(total[None], shape).astype(BF16)
    for copy in copies[2:]:
        copy.wait()


def select_kernel(got_ref, out_ref, lists_ref):
    lists = jnp.max(got_ref[:, pl.ds(2 * TILES * SLICE, SLICE), :].astype(F32), axis=1).astype(jnp.int32)
    lists_ref[...] = lists
    chips = out_ref.shape[0]
    for group in range(chips // 2):
        for slot in range(8):
            for row, column in ((0, slot % 4), (SLICE, slot % 4 + 4)):
                block = lists[2 * group + slot // 4, column]
                owner = lax.shift_right_logical(block, 1)
                first = row * TILES + (block & 1) * (2 * SLICE)
                for tile in range(2):
                    rows = pl.ds(pl.multiple_of(first + tile * SLICE, SLICE), SLICE)
                    piece = got_ref[owner, rows, :]
                    lanes = pl.ds(tile * LANES, LANES)
                    out_ref[group, slot, pl.ds(row, SLICE), lanes] = piece
                    out_ref[group + chips // 2, slot, pl.ds(row, SLICE), lanes] = piece


def dot(a, b, da, db):
    return lax.dot_general(a, b, (((da,), (db,)), ((), ())), preferred_element_type=F32)


def slots_of(j):
    core = lax.axis_index("mp") & 1
    return [4 * core + (j ^ m) for m in (0, 1, 2)] + [4 * (1 - core) + j]


def block_of(ref, row, slot):
    return ref[:, slot, pl.ds(row, SLICE), :].reshape(-1, SIDE)


def activations(ref, win_ref, wout_ref, j):
    slots = slots_of(j)
    pre = sum(dot(block_of(ref, 0, slots[k]), win_ref[j, k], 1, 0) for k in range(4))
    d_act = sum(dot(block_of(ref, SLICE, slots[k]), wout_ref[j, k], 1, 1) for k in range(4))
    c = math.sqrt(2.0 / math.pi)
    square = pre * pre
    th = jnp.tanh(c * (pre + 0.044715 * (square * pre)))
    half = 0.5 * (1.0 + th)
    slope = half + (0.5 * c) * pre * (1.0 - th * th) * (1.0 + (3 * 0.044715) * square)
    return (pre * half).astype(BF16), (d_act * slope).astype(BF16)


def first_kernel(own_ref, win_ref, wout_ref, act_ref, dpre_ref):
    for j in range(4):
        lanes = pl.ds(j * SIDE, SIDE)
        act_ref[:, lanes], dpre_ref[:, lanes] = activations(own_ref, win_ref, wout_ref, j)


def hidden_kernel(
    own_ref, oth_ref, act_ref, dpre_ref, win_ref, wout_ref,
    grads_ref, all_act_ref, all_dpre_ref, held, sems,
):
    side = lax.axis_index("dp") & 1
    zs = held.shape[2]
    copies = []
    for j in range(4):
        lanes = pl.ds(j * SIDE, SIDE)
        act, d_pre = activations(oth_ref, win_ref, wout_ref, j)
        act = jnp.concatenate([act_ref[:, lanes], act], axis=0)
        d_pre = jnp.concatenate([dpre_ref[:, lanes], d_pre], axis=0)
        all_act_ref[:, lanes] = act
        all_dpre_ref[:, lanes] = d_pre
        for k, slot in enumerate(slots_of(j)):
            x = jnp.concatenate([block_of(own_ref, 0, slot), block_of(oth_ref, 0, slot)], axis=0)
            dy = jnp.concatenate([block_of(own_ref, SLICE, slot), block_of(oth_ref, SLICE, slot)], axis=0)
            g_in = dot(x, d_pre, 0, 0).astype(BF16).reshape(zs, 2, SLICE, SIDE)
            g_out = dot(act, dy, 0, 0).astype(BF16).reshape(zs, 2, SLICE, SIDE)
            for away in range(2):
                held[j, k, :, away ^ side, 0] = g_in[:, away]
                held[j, k, :, away ^ side, 1] = g_out[:, away]
            copies.append(pltpu.make_async_copy(held.at[j, k], grads_ref.at[:, :, :, j, k], sems.at[j, k]))
            copies[-1].start()
    for copy in copies:
        copy.wait()


def project_kernel(act_ref, dpre_ref, win_ref, wout_ref, own_ref, oth_ref):
    core = lax.axis_index("mp") & 1
    acts = [act_ref[:, t * SIDE : (t + 1) * SIDE] for t in range(4)]
    dpres = [dpre_ref[:, t * SIDE : (t + 1) * SIDE] for t in range(4)]

    def put(row, slot, total):
        pieces = total.astype(BF16).reshape(2, -1, SLICE, SIDE)
        own_ref[:, slot, pl.ds(row, SLICE), :] = pieces[0]
        oth_ref[:, slot, pl.ds(row, SLICE), :] = pieces[1]

    for s in range(4):
        near, far = 4 * core + s, 4 * (1 - core) + s
        three = [(k, s ^ m) for k, m in enumerate((0, 1, 2))]
        put(0, near, sum(dot(acts[j], wout_ref[j, k], 1, 0) for k, j in three))
        put(0, far, dot(acts[s], wout_ref[s, 3], 1, 0))
        put(SLICE, near, sum(dot(dpres[j], win_ref[j, k], 1, 1) for k, j in three))
        put(SLICE, far, dot(dpres[s], win_ref[s, 3], 1, 1))


def sort_kernel(table, got_ref, out_ref):
    chips = got_ref.shape[0]
    for group in range(chips // 2):
        for slot in range(8):
            for row, column in ((0, slot % 4 + 4), (SLICE, slot % 4)):
                block = table[2 * group + slot // 4, column]
                owner = lax.shift_right_logical(block, 1)
                half = pl.multiple_of((block & 1) * SIDE, SIDE)
                rows = pl.ds(row, SLICE)
                total = got_ref[group, slot, rows, :].astype(F32)
                total = total + got_ref[group + chips // 2, slot, rows, :].astype(F32)
                out_ref[owner, rows, pl.ds(half, SIDE)] = total.astype(BF16)


def fetch_kernel(sum_ref, own_ref, away_ref, sems):
    copies = [
        pltpu.make_async_copy(sum_ref.at[half], ref, sems.at[half])
        for half, ref in enumerate((own_ref, away_ref))
    ]
    for copy in copies:
        copy.start()
    for copy in copies:
        copy.wait()


def finish_kernel(scale, own_ref, came_ref, in_ref, out_ref, held, sems):
    copies = []
    for which, ref in enumerate((in_ref, out_ref)):
        held[which] = (own_ref[which].astype(F32) + came_ref[which].astype(F32)) * scale
        copies.append(pltpu.make_async_copy(held.at[which], ref, sems.at[which]))
        copies[-1].start()
    for copy in copies:
        copy.wait()


def shards(tokens, cotangent, w_in, w_out, in_blocks, out_blocks):
    n = lax.axis_size("mp")
    n_dp = lax.axis_size("dp")
    zs = n_dp // 2
    tok = tokens.shape[0]
    total_tok = tok * n_dp
    mate = [(i, i ^ 1) for i in range(n)]
    same_core = [[2 * chip + core for chip in range(n // 2)] for core in range(2)]

    packed = pl.pallas_call(
        pack_kernel,
        out_shape=jax.ShapeDtypeStruct((n, (2 * TILES + 1) * SLICE, LANES), BF16),
        in_specs=[HBM] * 4,
        out_specs=VMEM,
        scratch_shapes=[pltpu.VMEM((2, 4, 4), jnp.int32), pltpu.SemaphoreType.DMA((2 + 2 * TILES,))],
        compiler_params=params(),
        name="pack",
    )(
        in_hbm(tokens.reshape(n, SLICE, 2 * SIDE)),
        in_hbm(cotangent.reshape(n, SLICE, 2 * SIDE)),
        in_hbm(in_blocks),
        in_hbm(out_blocks),
    )
    got = lax.all_to_all(packed, "mp", 0, 0, tiled=True)
    share = jax.ShapeDtypeStruct((n // 2, 8, 2 * SLICE, SIDE), BF16)
    chosen, table = pl.pallas_call(
        select_kernel,
        out_shape=(share, jax.ShapeDtypeStruct((n, LANES), jnp.int32)),
        in_specs=[VMEM],
        out_specs=(VMEM, VMEM),
        compiler_params=params(),
        name="select",
    )(got)
    own = lax.all_to_all(chosen, "mp", 0, 0, axis_index_groups=same_core, tiled=True)
    oth = lax.ppermute(own, "mp", mate)

    half = jax.ShapeDtypeStruct((tok // 2, QUAD), BF16)
    first_act, first_dpre = pl.pallas_call(
        first_kernel,
        out_shape=(half, half),
        in_specs=[VMEM] * 3,
        out_specs=(VMEM, VMEM),
        compiler_params=params(),
        name="first",
    )(own, w_in, w_out)
    quad = jax.ShapeDtypeStruct((tok, QUAD), BF16)
    grads, act, d_pre = pl.pallas_call(
        hidden_kernel,
        out_shape=(pltpu.HBM((zs, 2, 2, 4, 4, SLICE, SIDE), BF16), quad, quad),
        in_specs=[VMEM] * 6,
        out_specs=(HBM, VMEM, VMEM),
        scratch_shapes=[
            pltpu.VMEM((4, 4, zs, 2, 2, SLICE, SIDE), BF16),
            pltpu.SemaphoreType.DMA((4, 4)),
        ],
        compiler_params=params(),
        name="hidden",
    )(own, oth, first_act, first_dpre, w_in, w_out)

    columns = [[z * 2 + xl for z in range(zs)] for xl in range(2)]
    grad_sum = lax.psum_scatter(
        grads.reshape(-1, SIDE), "dp", scatter_dimension=0, axis_index_groups=columns, tiled=True
    )

    part_own, part_oth = pl.pallas_call(
        project_kernel,
        out_shape=(share, share),
        in_specs=[VMEM] * 4,
        out_specs=(VMEM, VMEM),
        compiler_params=params(),
        name="project",
    )(act, d_pre, w_in, w_out)
    part_mate = lax.ppermute(part_oth, "mp", mate)
    part = (part_own.astype(F32) + part_mate.astype(F32)).astype(BF16)
    slices = lax.all_to_all(part, "mp", 0, 0, axis_index_groups=same_core, tiled=True)
    sorted_ = pl.pallas_call(
        sort_kernel,
        out_shape=jax.ShapeDtypeStruct((n, 2 * SLICE, 2 * SIDE), BF16),
        in_specs=[SMEM, VMEM],
        out_specs=VMEM,
        compiler_params=params(),
        name="sort",
    )(table, slices)
    final = lax.all_to_all(sorted_, "mp", 0, 0, tiled=True)
    output = final[:, :SLICE].reshape(tok, 2 * SIDE)
    grad_tokens = final[:, SLICE:].reshape(tok, 2 * SIDE)

    grad_sum, output, grad_tokens = lax.optimization_barrier((grad_sum, output, grad_tokens))
    halves = grad_sum.reshape(2, 2, 4, 4, SLICE, SIDE)
    half = jax.ShapeDtypeStruct((2, 4, 4, SLICE, SIDE), BF16)
    mine, away = pl.pallas_call(
        fetch_kernel,
        out_shape=(half, half),
        in_specs=[HBM],
        out_specs=(VMEM, VMEM),
        scratch_shapes=[pltpu.SemaphoreType.DMA((2,))],
        compiler_params=params(),
        name="fetch",
    )(in_hbm(halves))
    came = lax.ppermute(away, "dp", [(i, i ^ 1) for i in range(n_dp)])
    grad_shape = pltpu.HBM((4, 4, SLICE, SIDE), F32)
    grad_in, grad_out = pl.pallas_call(
        functools.partial(finish_kernel, 1.0 / math.sqrt(total_tok)),
        out_shape=(grad_shape, grad_shape),
        in_specs=[VMEM, VMEM],
        out_specs=(HBM, HBM),
        scratch_shapes=[
            pltpu.VMEM((2, 4, 4, SLICE, SIDE), F32),
            pltpu.SemaphoreType.DMA((2,)),
        ],
        compiler_params=params(),
        name="finish",
    )(mine, came)
    return output, grad_tokens, grad_in, grad_out


def solution(mesh):
    placed = (
        P("dp", "mp"),
        P("dp", "mp"),
        P("mp", None, None, None),
        P("mp", None, None, None),
        P("mp", None),
        P("mp", None),
    )
    return jax.shard_map(
        shards,
        mesh=mesh,
        in_specs=placed,
        out_specs=(
            P("dp", "mp"),
            P("dp", "mp"),
            P("mp", None, "dp", None),
            P("mp", None, "dp", None),
        ),
        check_vma=False,
    )
```

```python
import functools
import math

import jax
import jax.numpy as jnp
from jax import lax
from jax.experimental import pallas as pl
from jax.experimental.pallas import tpu as pltpu
from jax.sharding import PartitionSpec as P

SIDE = 256
QUAD = 4 * SIDE
SLICE = 16
LANES = 128
TILES = 2 * SIDE // LANES
VMEM = pl.BlockSpec(memory_space=pltpu.VMEM)
HBM = pl.BlockSpec(memory_space=pltpu.HBM)
SMEM = pl.BlockSpec(memory_space=pltpu.SMEM)
BF16 = jnp.bfloat16
F32 = jnp.float32


def in_hbm(array):
    return pltpu.with_memory_space_constraint(array, pltpu.HBM)


def params():
    return pltpu.CompilerParams(vmem_limit_bytes=40 * 1024 * 1024)


def pack_kernel(x_ref, dy_ref, p_ref, q_ref, out_ref, lists, sems):
    copies = [
        pltpu.make_async_copy(p_ref, lists.at[0], sems.at[0]),
        pltpu.make_async_copy(q_ref, lists.at[1], sems.at[1]),
    ]
    for part, ref in enumerate((x_ref, dy_ref)):
        for tile in range(TILES):
            at = part * TILES + tile
            source = ref.at[:, :, pl.ds(tile * LANES, LANES)]
            target = out_ref.at[:, pl.ds(at * SLICE, SLICE), :]
            copies.append(pltpu.make_async_copy(source, target, sems.at[2 + at]))
    for copy in copies:
        copy.start()
    row = lax.broadcasted_iota(jnp.int32, (4, LANES), 0)
    lane = lax.broadcasted_iota(jnp.int32, (4, LANES), 1)
    total = jnp.zeros((1, LANES), F32)
    for part in range(2):
        copies[part].wait()
        column = jnp.broadcast_to(lists[part][:, 0:1], (4, LANES)).astype(F32)
        total = total + jnp.sum(jnp.where(lane == row + 4 * part, column, 0.0), axis=0, keepdims=True)
    shape = (out_ref.shape[0], SLICE, LANES)
    out_ref[:, pl.ds(2 * TILES * SLICE, SLICE), :] = jnp.broadcast_to(total[None], shape).astype(BF16)
    for copy in copies[2:]:
        copy.wait()


def select_kernel(got_ref, out_ref, lists_ref):
    lists = jnp.max(got_ref[:, pl.ds(2 * TILES * SLICE, SLICE), :].astype(F32), axis=1).astype(jnp.int32)
    lists_ref[...] = lists
    chips = out_ref.shape[0]
    for group in range(chips // 2):
        for slot in range(8):
            for row, column in ((0, slot % 4), (SLICE, slot % 4 + 4)):
                block = lists[2 * group + slot // 4, column]
                owner = lax.shift_right_logical(block, 1)
                first = row * TILES + (block & 1) * (2 * SLICE)
                for tile in range(2):
                    rows = pl.ds(pl.multiple_of(first + tile * SLICE, SLICE), SLICE)
                    piece = got_ref[owner, rows, :]
                    lanes = pl.ds(tile * LANES, LANES)
                    out_ref[group, slot, pl.ds(row, SLICE), lanes] = piece
                    out_ref[group + chips // 2, slot, pl.ds(row, SLICE), lanes] = piece


def dot(a, b, da, db):
    return lax.dot_general(a, b, (((da,), (db,)), ((), ())), preferred_element_type=F32)


def slots_of(j):
    core = lax.axis_index("mp") & 1
    return [4 * core + (j ^ m) for m in (0, 1, 2)] + [4 * (1 - core) + j]


def block_of(ref, row, slot):
    return ref[:, slot, pl.ds(row, SLICE), :].reshape(-1, SIDE)


def activations(ref, win_ref, wout_ref, j):
    slots = slots_of(j)
    pre = sum(dot(block_of(ref, 0, slots[k]), win_ref[j, k], 1, 0) for k in range(4))
    d_act = sum(dot(block_of(ref, SLICE, slots[k]), wout_ref[j, k], 1, 1) for k in range(4))
    c = math.sqrt(2.0 / math.pi)
    square = pre * pre
    th = jnp.tanh(c * (pre + 0.044715 * (square * pre)))
    half = 0.5 * (1.0 + th)
    slope = half + (0.5 * c) * pre * (1.0 - th * th) * (1.0 + (3 * 0.044715) * square)
    return (pre * half).astype(BF16), (d_act * slope).astype(BF16)


def first_kernel(own_ref, win_ref, wout_ref, act_ref, dpre_ref):
    for j in range(4):
        lanes = pl.ds(j * SIDE, SIDE)
        act_ref[:, lanes], dpre_ref[:, lanes] = activations(own_ref, win_ref, wout_ref, j)


def hidden_kernel(
    own_ref, oth_ref, act_ref, dpre_ref, win_ref, wout_ref,
    grads_ref, more_act_ref, more_dpre_ref, held, sems,
):
    side = lax.axis_index("dp") & 1
    zs = held.shape[2]
    copies = []
    for j in range(4):
        lanes = pl.ds(j * SIDE, SIDE)
        act, d_pre = activations(oth_ref, win_ref, wout_ref, j)
        more_act_ref[:, lanes] = act
        more_dpre_ref[:, lanes] = d_pre
        act = jnp.concatenate([act_ref[:, lanes], act], axis=0)
        d_pre = jnp.concatenate([dpre_ref[:, lanes], d_pre], axis=0)
        for k, slot in enumerate(slots_of(j)):
            x = jnp.concatenate([block_of(own_ref, 0, slot), block_of(oth_ref, 0, slot)], axis=0)
            dy = jnp.concatenate([block_of(own_ref, SLICE, slot), block_of(oth_ref, SLICE, slot)], axis=0)
            g_in = dot(x, d_pre, 0, 0).astype(BF16).reshape(zs, 2, SLICE, SIDE)
            g_out = dot(act, dy, 0, 0).astype(BF16).reshape(zs, 2, SLICE, SIDE)
            for away in range(2):
                held[j, k, :, away ^ side, 0] = g_in[:, away]
                held[j, k, :, away ^ side, 1] = g_out[:, away]
            copies.append(pltpu.make_async_copy(held.at[j, k], grads_ref.at[:, :, :, j, k], sems.at[j, k]))
            copies[-1].start()
    for copy in copies:
        copy.wait()


def project_kernel(
    act_ref, dpre_ref, more_act_ref, more_dpre_ref, win_ref, wout_ref, own_ref, oth_ref
):
    core = lax.axis_index("mp") & 1

    def joined(first_ref, more_ref, t):
        lanes = pl.ds(t * SIDE, SIDE)
        return jnp.concatenate([first_ref[:, lanes], more_ref[:, lanes]], axis=0)

    acts = [joined(act_ref, more_act_ref, t) for t in range(4)]
    dpres = [joined(dpre_ref, more_dpre_ref, t) for t in range(4)]

    def put(row, slot, total):
        pieces = total.astype(BF16).reshape(2, -1, SLICE, SIDE)
        own_ref[:, slot, pl.ds(row, SLICE), :] = pieces[0]
        oth_ref[:, slot, pl.ds(row, SLICE), :] = pieces[1]

    for s in range(4):
        near, far = 4 * core + s, 4 * (1 - core) + s
        three = [(k, s ^ m) for k, m in enumerate((0, 1, 2))]
        put(0, near, sum(dot(acts[j], wout_ref[j, k], 1, 0) for k, j in three))
        put(0, far, dot(acts[s], wout_ref[s, 3], 1, 0))
        put(SLICE, near, sum(dot(dpres[j], win_ref[j, k], 1, 1) for k, j in three))
        put(SLICE, far, dot(dpres[s], win_ref[s, 3], 1, 1))


def sort_kernel(table, got_ref, out_ref):
    chips = got_ref.shape[0]
    for group in range(chips // 2):
        for slot in range(8):
            for row, column in ((0, slot % 4 + 4), (SLICE, slot % 4)):
                block = table[2 * group + slot // 4, column]
                owner = lax.shift_right_logical(block, 1)
                half = pl.multiple_of((block & 1) * SIDE, SIDE)
                rows = pl.ds(row, SLICE)
                total = got_ref[group, slot, rows, :].astype(F32)
                total = total + got_ref[group + chips // 2, slot, rows, :].astype(F32)
                out_ref[owner, rows, pl.ds(half, SIDE)] = total.astype(BF16)


def fetch_kernel(which, sum_ref, half_ref, sem):
    copy = pltpu.make_async_copy(sum_ref.at[which], half_ref, sem)
    copy.start()
    copy.wait()


def finish_kernel(scale, own_ref, came_ref, in_ref, out_ref, held, sems):
    copies = []
    for which, ref in enumerate((in_ref, out_ref)):
        held[which] = (own_ref[which].astype(F32) + came_ref[which].astype(F32)) * scale
        copies.append(pltpu.make_async_copy(held.at[which], ref, sems.at[which]))
        copies[-1].start()
    for copy in copies:
        copy.wait()


def shards(tokens, cotangent, w_in, w_out, in_blocks, out_blocks):
    n = lax.axis_size("mp")
    n_dp = lax.axis_size("dp")
    zs = n_dp // 2
    tok = tokens.shape[0]
    total_tok = tok * n_dp
    mate = [(i, i ^ 1) for i in range(n)]
    same_core = [[2 * chip + core for chip in range(n // 2)] for core in range(2)]

    packed = pl.pallas_call(
        pack_kernel,
        out_shape=jax.ShapeDtypeStruct((n, (2 * TILES + 1) * SLICE, LANES), BF16),
        in_specs=[HBM] * 4,
        out_specs=VMEM,
        scratch_shapes=[pltpu.VMEM((2, 4, 4), jnp.int32), pltpu.SemaphoreType.DMA((2 + 2 * TILES,))],
        compiler_params=params(),
        name="pack",
    )(
        in_hbm(tokens.reshape(n, SLICE, 2 * SIDE)),
        in_hbm(cotangent.reshape(n, SLICE, 2 * SIDE)),
        in_hbm(in_blocks),
        in_hbm(out_blocks),
    )
    got = lax.all_to_all(packed, "mp", 0, 0, tiled=True)
    share = jax.ShapeDtypeStruct((n // 2, 8, 2 * SLICE, SIDE), BF16)
    chosen, table = pl.pallas_call(
        select_kernel,
        out_shape=(share, jax.ShapeDtypeStruct((n, LANES), jnp.int32)),
        in_specs=[VMEM],
        out_specs=(VMEM, VMEM),
        compiler_params=params(),
        name="select",
    )(got)
    own = lax.all_to_all(chosen, "mp", 0, 0, axis_index_groups=same_core, tiled=True)
    oth = lax.ppermute(own, "mp", mate)

    half = jax.ShapeDtypeStruct((tok // 2, QUAD), BF16)
    first_act, first_dpre = pl.pallas_call(
        first_kernel,
        out_shape=(half, half),
        in_specs=[VMEM] * 3,
        out_specs=(VMEM, VMEM),
        compiler_params=params(),
        name="first",
    )(own, w_in, w_out)
    grads, more_act, more_dpre = pl.pallas_call(
        hidden_kernel,
        out_shape=(pltpu.HBM((zs, 2, 2, 4, 4, SLICE, SIDE), BF16), half, half),
        in_specs=[VMEM] * 6,
        out_specs=(HBM, VMEM, VMEM),
        scratch_shapes=[
            pltpu.VMEM((4, 4, zs, 2, 2, SLICE, SIDE), BF16),
            pltpu.SemaphoreType.DMA((4, 4)),
        ],
        compiler_params=params(),
        name="hidden",
    )(own, oth, first_act, first_dpre, w_in, w_out)

    columns = [[z * 2 + xl for z in range(zs)] for xl in range(2)]
    grad_sum = lax.psum_scatter(
        grads.reshape(-1, SIDE), "dp", scatter_dimension=0, axis_index_groups=columns, tiled=True
    )

    part_own, part_oth = pl.pallas_call(
        project_kernel,
        out_shape=(share, share),
        in_specs=[VMEM] * 6,
        out_specs=(VMEM, VMEM),
        compiler_params=params(),
        name="project",
    )(first_act, first_dpre, more_act, more_dpre, w_in, w_out)
    part_mate = lax.ppermute(part_oth, "mp", mate)
    part = (part_own.astype(F32) + part_mate.astype(F32)).astype(BF16)
    slices = lax.all_to_all(part, "mp", 0, 0, axis_index_groups=same_core, tiled=True)
    sorted_ = pl.pallas_call(
        sort_kernel,
        out_shape=jax.ShapeDtypeStruct((n, 2 * SLICE, 2 * SIDE), BF16),
        in_specs=[SMEM, VMEM],
        out_specs=VMEM,
        compiler_params=params(),
        name="sort",
    )(table, slices)
    final = lax.all_to_all(sorted_, "mp", 0, 0, tiled=True)
    output = final[:, :SLICE].reshape(tok, 2 * SIDE)
    grad_tokens = final[:, SLICE:].reshape(tok, 2 * SIDE)

    grad_sum, output, grad_tokens = lax.optimization_barrier((grad_sum, output, grad_tokens))
    halves = grad_sum.reshape(2, 2, 4, 4, SLICE, SIDE)
    summed = in_hbm(halves)
    fetch = lambda which, name: pl.pallas_call(
        functools.partial(fetch_kernel, which),
        out_shape=jax.ShapeDtypeStruct((2, 4, 4, SLICE, SIDE), BF16),
        in_specs=[HBM],
        out_specs=VMEM,
        scratch_shapes=[pltpu.SemaphoreType.DMA],
        compiler_params=params(),
        name=name,
    )(summed)
    came = lax.ppermute(fetch(1, "fetch_away"), "dp", [(i, i ^ 1) for i in range(n_dp)])
    mine = fetch(0, "fetch_own")
    grad_shape = pltpu.HBM((4, 4, SLICE, SIDE), F32)
    grad_in, grad_out = pl.pallas_call(
        functools.partial(finish_kernel, 1.0 / math.sqrt(total_tok)),
        out_shape=(grad_shape, grad_shape),
        in_specs=[VMEM, VMEM],
        out_specs=(HBM, HBM),
        scratch_shapes=[
            pltpu.VMEM((2, 4, 4, SLICE, SIDE), F32),
            pltpu.SemaphoreType.DMA((2,)),
        ],
        compiler_params=params(),
        name="finish",
    )(mine, came)
    return output, grad_tokens, grad_in, grad_out


def solution(mesh):
    placed = (
        P("dp", "mp"),
        P("dp", "mp"),
        P("mp", None, None, None),
        P("mp", None, None, None),
        P("mp", None),
        P("mp", None),
    )
    return jax.shard_map(
        shards,
        mesh=mesh,
        in_specs=placed,
        out_specs=(
            P("dp", "mp"),
            P("dp", "mp"),
            P("mp", None, "dp", None),
            P("mp", None, "dp", None),
        ),
        check_vma=False,
    )
```

```python
import functools
import math

import jax
import jax.numpy as jnp
from jax import lax
from jax.experimental import pallas as pl
from jax.experimental.pallas import tpu as pltpu
from jax.sharding import PartitionSpec as P

SIDE = 256
QUAD = 4 * SIDE
SLICE = 16
LANES = 128
TILES = 2 * SIDE // LANES
VMEM = pl.BlockSpec(memory_space=pltpu.VMEM)
HBM = pl.BlockSpec(memory_space=pltpu.HBM)
SMEM = pl.BlockSpec(memory_space=pltpu.SMEM)
BF16 = jnp.bfloat16
F32 = jnp.float32


def in_hbm(array):
    return pltpu.with_memory_space_constraint(array, pltpu.HBM)


def params():
    return pltpu.CompilerParams(vmem_limit_bytes=40 * 1024 * 1024)


def pack_kernel(x_ref, dy_ref, p_ref, q_ref, out_ref, lists, sems):
    copies = [
        pltpu.make_async_copy(p_ref, lists.at[0], sems.at[0]),
        pltpu.make_async_copy(q_ref, lists.at[1], sems.at[1]),
    ]
    for part, ref in enumerate((x_ref, dy_ref)):
        for tile in range(TILES):
            at = part * TILES + tile
            source = ref.at[:, :, pl.ds(tile * LANES, LANES)]
            target = out_ref.at[:, pl.ds(at * SLICE, SLICE), :]
            copies.append(pltpu.make_async_copy(source, target, sems.at[2 + at]))
    for copy in copies:
        copy.start()
    row = lax.broadcasted_iota(jnp.int32, (4, LANES), 0)
    lane = lax.broadcasted_iota(jnp.int32, (4, LANES), 1)
    total = jnp.zeros((1, LANES), F32)
    for part in range(2):
        copies[part].wait()
        column = jnp.broadcast_to(lists[part][:, 0:1], (4, LANES)).astype(F32)
        total = total + jnp.sum(jnp.where(lane == row + 4 * part, column, 0.0), axis=0, keepdims=True)
    shape = (out_ref.shape[0], SLICE, LANES)
    out_ref[:, pl.ds(2 * TILES * SLICE, SLICE), :] = jnp.broadcast_to(total[None], shape).astype(BF16)
    for copy in copies[2:]:
        copy.wait()


def select_kernel(got_ref, out_ref, lists_ref):
    lists = jnp.max(got_ref[:, pl.ds(2 * TILES * SLICE, SLICE), :].astype(F32), axis=1).astype(jnp.int32)
    lists_ref[...] = lists
    chips = out_ref.shape[0]
    for group in range(chips // 2):
        for slot in range(8):
            for row, column in ((0, slot % 4), (SLICE, slot % 4 + 4)):
                block = lists[2 * group + slot // 4, column]
                owner = lax.shift_right_logical(block, 1)
                first = row * TILES + (block & 1) * (2 * SLICE)
                for tile in range(2):
                    rows = pl.ds(pl.multiple_of(first + tile * SLICE, SLICE), SLICE)
                    piece = got_ref[owner, rows, :]
                    lanes = pl.ds(tile * LANES, LANES)
                    out_ref[group, slot, pl.ds(row, SLICE), lanes] = piece
                    out_ref[group + chips // 2, slot, pl.ds(row, SLICE), lanes] = piece


def dot(a, b, da, db):
    return lax.dot_general(a, b, (((da,), (db,)), ((), ())), preferred_element_type=F32)


def slots_of(j):
    core = lax.axis_index("mp") & 1
    return [4 * core + (j ^ m) for m in (0, 1, 2)] + [4 * (1 - core) + j]


def block_of(ref, row, slot):
    return ref[:, slot, pl.ds(row, SLICE), :].reshape(-1, SIDE)


def activations(ref, win_ref, wout_ref, j):
    slots = slots_of(j)
    pre = sum(dot(block_of(ref, 0, slots[k]), win_ref[j, k], 1, 0) for k in range(4))
    d_act = sum(dot(block_of(ref, SLICE, slots[k]), wout_ref[j, k], 1, 1) for k in range(4))
    c = math.sqrt(2.0 / math.pi)
    square = pre * pre
    th = jnp.tanh(c * (pre + 0.044715 * (square * pre)))
    half = 0.5 * (1.0 + th)
    slope = half + (0.5 * c) * pre * (1.0 - th * th) * (1.0 + (3 * 0.044715) * square)
    return (pre * half).astype(BF16), (d_act * slope).astype(BF16)


def first_kernel(own_ref, win_ref, wout_ref, act_ref, dpre_ref):
    for j in range(4):
        lanes = pl.ds(j * SIDE, SIDE)
        act_ref[:, lanes], dpre_ref[:, lanes] = activations(own_ref, win_ref, wout_ref, j)


def hidden_kernel(
    own_ref, oth_ref, act_ref, dpre_ref, win_ref, wout_ref,
    grads_ref, more_act_ref, more_dpre_ref, held, sems,
):
    side = lax.axis_index("dp") & 1
    zs = held.shape[2]
    copies = []
    made = []
    for j in range(4):
        lanes = pl.ds(j * SIDE, SIDE)
        act, d_pre = activations(oth_ref, win_ref, wout_ref, j)
        more_act_ref[:, lanes] = act
        more_dpre_ref[:, lanes] = d_pre
        act = jnp.concatenate([act_ref[:, lanes], act], axis=0)
        made.append((act, jnp.concatenate([dpre_ref[:, lanes], d_pre], axis=0)))
    for j, (act, d_pre) in enumerate(made):
        for k, slot in enumerate(slots_of(j)):
            x = jnp.concatenate([block_of(own_ref, 0, slot), block_of(oth_ref, 0, slot)], axis=0)
            dy = jnp.concatenate([block_of(own_ref, SLICE, slot), block_of(oth_ref, SLICE, slot)], axis=0)
            g_in = dot(x, d_pre, 0, 0).astype(BF16).reshape(zs, 2, SLICE, SIDE)
            g_out = dot(act, dy, 0, 0).astype(BF16).reshape(zs, 2, SLICE, SIDE)
            for away in range(2):
                held[j, k, :, away ^ side, 0] = g_in[:, away]
                held[j, k, :, away ^ side, 1] = g_out[:, away]
            copies.append(pltpu.make_async_copy(held.at[j, k], grads_ref.at[:, :, :, j, k], sems.at[j, k]))
            copies[-1].start()
    for copy in copies:
        copy.wait()


def project_kernel(
    act_ref, dpre_ref, more_act_ref, more_dpre_ref, win_ref, wout_ref, own_ref, oth_ref
):
    core = lax.axis_index("mp") & 1

    def joined(first_ref, more_ref, t):
        lanes = pl.ds(t * SIDE, SIDE)
        return jnp.concatenate([first_ref[:, lanes], more_ref[:, lanes]], axis=0)

    acts = [joined(act_ref, more_act_ref, t) for t in range(4)]
    dpres = [joined(dpre_ref, more_dpre_ref, t) for t in range(4)]

    def put(row, slot, total):
        pieces = total.astype(BF16).reshape(2, -1, SLICE, SIDE)
        own_ref[:, slot, pl.ds(row, SLICE), :] = pieces[0]
        oth_ref[:, slot, pl.ds(row, SLICE), :] = pieces[1]

    for s in range(4):
        near, far = 4 * core + s, 4 * (1 - core) + s
        three = [(k, s ^ m) for k, m in enumerate((0, 1, 2))]
        put(0, near, sum(dot(acts[j], wout_ref[j, k], 1, 0) for k, j in three))
        put(0, far, dot(acts[s], wout_ref[s, 3], 1, 0))
        put(SLICE, near, sum(dot(dpres[j], win_ref[j, k], 1, 1) for k, j in three))
        put(SLICE, far, dot(dpres[s], win_ref[s, 3], 1, 1))


def sort_kernel(table, got_ref, out_ref):
    chips = got_ref.shape[0]
    for group in range(chips // 2):
        for slot in range(8):
            for row, column in ((0, slot % 4 + 4), (SLICE, slot % 4)):
                block = table[2 * group + slot // 4, column]
                owner = lax.shift_right_logical(block, 1)
                half = pl.multiple_of((block & 1) * SIDE, SIDE)
                rows = pl.ds(row, SLICE)
                total = got_ref[group, slot, rows, :].astype(F32)
                total = total + got_ref[group + chips // 2, slot, rows, :].astype(F32)
                out_ref[owner, rows, pl.ds(half, SIDE)] = total.astype(BF16)


def fetch_kernel(which, sum_ref, half_ref, sem):
    copy = pltpu.make_async_copy(sum_ref.at[which], half_ref, sem)
    copy.start()
    copy.wait()


def finish_kernel(scale, own_ref, came_ref, in_ref, out_ref, held, sems):
    copies = []
    for which, ref in enumerate((in_ref, out_ref)):
        held[which] = (own_ref[which].astype(F32) + came_ref[which].astype(F32)) * scale
        copies.append(pltpu.make_async_copy(held.at[which], ref, sems.at[which]))
        copies[-1].start()
    for copy in copies:
        copy.wait()


def shards(tokens, cotangent, w_in, w_out, in_blocks, out_blocks):
    n = lax.axis_size("mp")
    n_dp = lax.axis_size("dp")
    zs = n_dp // 2
    tok = tokens.shape[0]
    total_tok = tok * n_dp
    mate = [(i, i ^ 1) for i in range(n)]
    same_core = [[2 * chip + core for chip in range(n // 2)] for core in range(2)]

    packed = pl.pallas_call(
        pack_kernel,
        out_shape=jax.ShapeDtypeStruct((n, (2 * TILES + 1) * SLICE, LANES), BF16),
        in_specs=[HBM] * 4,
        out_specs=VMEM,
        scratch_shapes=[pltpu.VMEM((2, 4, 4), jnp.int32), pltpu.SemaphoreType.DMA((2 + 2 * TILES,))],
        compiler_params=params(),
        name="pack",
    )(
        in_hbm(tokens.reshape(n, SLICE, 2 * SIDE)),
        in_hbm(cotangent.reshape(n, SLICE, 2 * SIDE)),
        in_hbm(in_blocks),
        in_hbm(out_blocks),
    )
    got = lax.all_to_all(packed, "mp", 0, 0, tiled=True)
    share = jax.ShapeDtypeStruct((n // 2, 8, 2 * SLICE, SIDE), BF16)
    chosen, table = pl.pallas_call(
        select_kernel,
        out_shape=(share, jax.ShapeDtypeStruct((n, LANES), jnp.int32)),
        in_specs=[VMEM],
        out_specs=(VMEM, VMEM),
        compiler_params=params(),
        name="select",
    )(got)
    own = lax.all_to_all(chosen, "mp", 0, 0, axis_index_groups=same_core, tiled=True)
    oth = lax.ppermute(own, "mp", mate)

    half = jax.ShapeDtypeStruct((tok // 2, QUAD), BF16)
    first_act, first_dpre = pl.pallas_call(
        first_kernel,
        out_shape=(half, half),
        in_specs=[VMEM] * 3,
        out_specs=(VMEM, VMEM),
        compiler_params=params(),
        name="first",
    )(own, w_in, w_out)
    grads, more_act, more_dpre = pl.pallas_call(
        hidden_kernel,
        out_shape=(pltpu.HBM((zs, 2, 2, 4, 4, SLICE, SIDE), BF16), half, half),
        in_specs=[VMEM] * 6,
        out_specs=(HBM, VMEM, VMEM),
        scratch_shapes=[
            pltpu.VMEM((4, 4, zs, 2, 2, SLICE, SIDE), BF16),
            pltpu.SemaphoreType.DMA((4, 4)),
        ],
        compiler_params=params(),
        name="hidden",
    )(own, oth, first_act, first_dpre, w_in, w_out)

    columns = [[z * 2 + xl for z in range(zs)] for xl in range(2)]
    grad_sum = lax.psum_scatter(
        grads.reshape(-1, SIDE), "dp", scatter_dimension=0, axis_index_groups=columns, tiled=True
    )

    part_own, part_oth = pl.pallas_call(
        project_kernel,
        out_shape=(share, share),
        in_specs=[VMEM] * 6,
        out_specs=(VMEM, VMEM),
        compiler_params=params(),
        name="project",
    )(first_act, first_dpre, more_act, more_dpre, w_in, w_out)
    part_mate = lax.ppermute(part_oth, "mp", mate)
    part = (part_own.astype(F32) + part_mate.astype(F32)).astype(BF16)
    slices = lax.all_to_all(part, "mp", 0, 0, axis_index_groups=same_core, tiled=True)
    sorted_ = pl.pallas_call(
        sort_kernel,
        out_shape=jax.ShapeDtypeStruct((n, 2 * SLICE, 2 * SIDE), BF16),
        in_specs=[SMEM, VMEM],
        out_specs=VMEM,
        compiler_params=params(),
        name="sort",
    )(table, slices)
    final = lax.all_to_all(sorted_, "mp", 0, 0, tiled=True)
    output = final[:, :SLICE].reshape(tok, 2 * SIDE)
    grad_tokens = final[:, SLICE:].reshape(tok, 2 * SIDE)

    grad_sum, output, grad_tokens = lax.optimization_barrier((grad_sum, output, grad_tokens))
    halves = grad_sum.reshape(2, 2, 4, 4, SLICE, SIDE)
    summed = in_hbm(halves)
    fetch = lambda which, name: pl.pallas_call(
        functools.partial(fetch_kernel, which),
        out_shape=jax.ShapeDtypeStruct((2, 4, 4, SLICE, SIDE), BF16),
        in_specs=[HBM],
        out_specs=VMEM,
        scratch_shapes=[pltpu.SemaphoreType.DMA],
        compiler_params=params(),
        name=name,
    )(summed)
    came = lax.ppermute(fetch(1, "fetch_away"), "dp", [(i, i ^ 1) for i in range(n_dp)])
    mine = fetch(0, "fetch_own")
    grad_shape = pltpu.HBM((4, 4, SLICE, SIDE), F32)
    grad_in, grad_out = pl.pallas_call(
        functools.partial(finish_kernel, 1.0 / math.sqrt(total_tok)),
        out_shape=(grad_shape, grad_shape),
        in_specs=[VMEM, VMEM],
        out_specs=(HBM, HBM),
        scratch_shapes=[
            pltpu.VMEM((2, 4, 4, SLICE, SIDE), F32),
            pltpu.SemaphoreType.DMA((2,)),
        ],
        compiler_params=params(),
        name="finish",
    )(mine, came)
    return output, grad_tokens, grad_in, grad_out


def solution(mesh):
    placed = (
        P("dp", "mp"),
        P("dp", "mp"),
        P("mp", None, None, None),
        P("mp", None, None, None),
        P("mp", None),
        P("mp", None),
    )
    return jax.shard_map(
        shards,
        mesh=mesh,
        in_specs=placed,
        out_specs=(
            P("dp", "mp"),
            P("dp", "mp"),
            P("mp", None, "dp", None),
            P("mp", None, "dp", None),
        ),
        check_vma=False,
    )
```

```python
import functools
import math

import jax
import jax.numpy as jnp
from jax import lax
from jax.experimental import pallas as pl
from jax.experimental.pallas import tpu as pltpu
from jax.sharding import PartitionSpec as P

SIDE = 256
QUAD = 4 * SIDE
SLICE = 16
LANES = 128
TILES = 2 * SIDE // LANES
VMEM = pl.BlockSpec(memory_space=pltpu.VMEM)
HBM = pl.BlockSpec(memory_space=pltpu.HBM)
SMEM = pl.BlockSpec(memory_space=pltpu.SMEM)
BF16 = jnp.bfloat16
F32 = jnp.float32


def in_hbm(array):
    return pltpu.with_memory_space_constraint(array, pltpu.HBM)


def params():
    return pltpu.CompilerParams(vmem_limit_bytes=40 * 1024 * 1024)


def pack_kernel(x_ref, dy_ref, p_ref, q_ref, out_ref, lists, sems):
    copies = [
        pltpu.make_async_copy(p_ref, lists.at[0], sems.at[0]),
        pltpu.make_async_copy(q_ref, lists.at[1], sems.at[1]),
    ]
    for part, ref in enumerate((x_ref, dy_ref)):
        for tile in range(TILES):
            at = part * TILES + tile
            source = ref.at[:, :, pl.ds(tile * LANES, LANES)]
            target = out_ref.at[:, pl.ds(at * SLICE, SLICE), :]
            copies.append(pltpu.make_async_copy(source, target, sems.at[2 + at]))
    for copy in copies:
        copy.start()
    row = lax.broadcasted_iota(jnp.int32, (4, LANES), 0)
    lane = lax.broadcasted_iota(jnp.int32, (4, LANES), 1)
    total = jnp.zeros((1, LANES), F32)
    for part in range(2):
        copies[part].wait()
        column = jnp.broadcast_to(lists[part][:, 0:1], (4, LANES)).astype(F32)
        total = total + jnp.sum(jnp.where(lane == row + 4 * part, column, 0.0), axis=0, keepdims=True)
    shape = (out_ref.shape[0], SLICE, LANES)
    out_ref[:, pl.ds(2 * TILES * SLICE, SLICE), :] = jnp.broadcast_to(total[None], shape).astype(BF16)
    for copy in copies[2:]:
        copy.wait()


def select_kernel(got_ref, out_ref, lists_ref):
    lists = jnp.max(got_ref[:, pl.ds(2 * TILES * SLICE, SLICE), :].astype(F32), axis=1).astype(jnp.int32)
    lists_ref[...] = lists
    chips = out_ref.shape[0]
    for group in range(chips // 2):
        for slot in range(8):
            for row, column in ((0, slot % 4), (SLICE, slot % 4 + 4)):
                block = lists[2 * group + slot // 4, column]
                owner = lax.shift_right_logical(block, 1)
                first = row * TILES + (block & 1) * (2 * SLICE)
                for tile in range(2):
                    rows = pl.ds(pl.multiple_of(first + tile * SLICE, SLICE), SLICE)
                    piece = got_ref[owner, rows, :]
                    lanes = pl.ds(tile * LANES, LANES)
                    out_ref[group, slot, pl.ds(row, SLICE), lanes] = piece
                    out_ref[group + chips // 2, slot, pl.ds(row, SLICE), lanes] = piece


def dot(a, b, da, db):
    return lax.dot_general(a, b, (((da,), (db,)), ((), ())), preferred_element_type=F32)


def slots_of(j):
    core = lax.axis_index("mp") & 1
    return [4 * core + (j ^ m) for m in (0, 1, 2)] + [4 * (1 - core) + j]


def block_of(ref, row, slot):
    return ref[:, slot, pl.ds(row, SLICE), :].reshape(-1, SIDE)


def activations(ref, win_ref, wout_ref, j):
    slots = slots_of(j)
    pre = sum(dot(block_of(ref, 0, slots[k]), win_ref[j, k], 1, 0) for k in range(4))
    d_act = sum(dot(block_of(ref, SLICE, slots[k]), wout_ref[j, k], 1, 1) for k in range(4))
    c = math.sqrt(2.0 / math.pi)
    square = pre * pre
    th = jnp.tanh(c * (pre + 0.044715 * (square * pre)))
    half = 0.5 * (1.0 + th)
    slope = half + (0.5 * c) * pre * (1.0 - th * th) * (1.0 + (3 * 0.044715) * square)
    return (pre * half).astype(BF16), (d_act * slope).astype(BF16)


def first_kernel(own_ref, win_ref, wout_ref, act_ref, dpre_ref):
    for j in range(4):
        lanes = pl.ds(j * SIDE, SIDE)
        act_ref[:, lanes], dpre_ref[:, lanes] = activations(own_ref, win_ref, wout_ref, j)


def hidden_kernel(
    own_ref, oth_ref, act_ref, dpre_ref, win_ref, wout_ref,
    grads_ref, more_act_ref, more_dpre_ref, held, sems,
):
    side = lax.axis_index("dp") & 1
    zs = held.shape[2]
    copies = []
    made = []
    for j in range(4):
        lanes = pl.ds(j * SIDE, SIDE)
        act, d_pre = activations(oth_ref, win_ref, wout_ref, j)
        more_act_ref[:, lanes] = act
        more_dpre_ref[:, lanes] = d_pre
        act = jnp.concatenate([act_ref[:, lanes], act], axis=0)
        made.append((act, jnp.concatenate([dpre_ref[:, lanes], d_pre], axis=0)))
    for j, (act, d_pre) in enumerate(made):
        for k, slot in enumerate(slots_of(j)):
            x = jnp.concatenate([block_of(own_ref, 0, slot), block_of(oth_ref, 0, slot)], axis=0)
            dy = jnp.concatenate([block_of(own_ref, SLICE, slot), block_of(oth_ref, SLICE, slot)], axis=0)
            g_in = dot(x, d_pre, 0, 0).astype(BF16).reshape(zs, 2, SLICE, SIDE)
            g_out = dot(act, dy, 0, 0).astype(BF16).reshape(zs, 2, SLICE, SIDE)
            for away in range(2):
                held[j, k, :, away ^ side, 0] = g_in[:, away]
                held[j, k, :, away ^ side, 1] = g_out[:, away]
            copies.append(pltpu.make_async_copy(held.at[j, k], grads_ref.at[:, :, :, j, k], sems.at[j, k]))
            copies[-1].start()
    for copy in copies:
        copy.wait()


def project_kernel(
    act_ref, dpre_ref, more_act_ref, more_dpre_ref, win_ref, wout_ref, own_ref, oth_ref
):
    core = lax.axis_index("mp") & 1

    def joined(first_ref, more_ref, t):
        lanes = pl.ds(t * SIDE, SIDE)
        return jnp.concatenate([first_ref[:, lanes], more_ref[:, lanes]], axis=0)

    acts = [joined(act_ref, more_act_ref, t) for t in range(4)]
    dpres = [joined(dpre_ref, more_dpre_ref, t) for t in range(4)]

    def put(row, slot, total):
        pieces = total.astype(BF16).reshape(2, -1, SLICE, SIDE)
        own_ref[:, slot, pl.ds(row, SLICE), :] = pieces[0]
        oth_ref[:, slot, pl.ds(row, SLICE), :] = pieces[1]

    for s in range(4):
        near, far = 4 * core + s, 4 * (1 - core) + s
        three = [(k, s ^ m) for k, m in enumerate((0, 1, 2))]
        put(0, near, sum(dot(acts[j], wout_ref[j, k], 1, 0) for k, j in three))
        put(0, far, dot(acts[s], wout_ref[s, 3], 1, 0))
        put(SLICE, near, sum(dot(dpres[j], win_ref[j, k], 1, 1) for k, j in three))
        put(SLICE, far, dot(dpres[s], win_ref[s, 3], 1, 1))


def sort_kernel(table, got_ref, out_ref):
    chips = got_ref.shape[0]
    for group in range(chips // 2):
        for slot in range(8):
            for row, column in ((0, slot % 4 + 4), (SLICE, slot % 4)):
                block = table[2 * group + slot // 4, column]
                owner = lax.shift_right_logical(block, 1)
                half = pl.multiple_of((block & 1) * SIDE, SIDE)
                rows = pl.ds(row, SLICE)
                total = got_ref[group, slot, rows, :].astype(F32)
                total = total + got_ref[group + chips // 2, slot, rows, :].astype(F32)
                out_ref[owner, rows, pl.ds(half, SIDE)] = total.astype(BF16)


def fetch_kernel(half, which, sum_ref, part_ref, sem):
    copy = pltpu.make_async_copy(sum_ref.at[half, which], part_ref, sem)
    copy.start()
    copy.wait()


def finish_kernel(scale, own_ref, came_ref, out_ref, held, sem):
    held[...] = (own_ref[...].astype(F32) + came_ref[...].astype(F32)) * scale
    copy = pltpu.make_async_copy(held, out_ref, sem)
    copy.start()
    copy.wait()


def shards(tokens, cotangent, w_in, w_out, in_blocks, out_blocks):
    n = lax.axis_size("mp")
    n_dp = lax.axis_size("dp")
    zs = n_dp // 2
    tok = tokens.shape[0]
    total_tok = tok * n_dp
    mate = [(i, i ^ 1) for i in range(n)]
    same_core = [[2 * chip + core for chip in range(n // 2)] for core in range(2)]

    packed = pl.pallas_call(
        pack_kernel,
        out_shape=jax.ShapeDtypeStruct((n, (2 * TILES + 1) * SLICE, LANES), BF16),
        in_specs=[HBM] * 4,
        out_specs=VMEM,
        scratch_shapes=[pltpu.VMEM((2, 4, 4), jnp.int32), pltpu.SemaphoreType.DMA((2 + 2 * TILES,))],
        compiler_params=params(),
        name="pack",
    )(
        in_hbm(tokens.reshape(n, SLICE, 2 * SIDE)),
        in_hbm(cotangent.reshape(n, SLICE, 2 * SIDE)),
        in_hbm(in_blocks),
        in_hbm(out_blocks),
    )
    got = lax.all_to_all(packed, "mp", 0, 0, tiled=True)
    share = jax.ShapeDtypeStruct((n // 2, 8, 2 * SLICE, SIDE), BF16)
    chosen, table = pl.pallas_call(
        select_kernel,
        out_shape=(share, jax.ShapeDtypeStruct((n, LANES), jnp.int32)),
        in_specs=[VMEM],
        out_specs=(VMEM, VMEM),
        compiler_params=params(),
        name="select",
    )(got)
    own = lax.all_to_all(chosen, "mp", 0, 0, axis_index_groups=same_core, tiled=True)
    oth = lax.ppermute(own, "mp", mate)

    half = jax.ShapeDtypeStruct((tok // 2, QUAD), BF16)
    first_act, first_dpre = pl.pallas_call(
        first_kernel,
        out_shape=(half, half),
        in_specs=[VMEM] * 3,
        out_specs=(VMEM, VMEM),
        compiler_params=params(),
        name="first",
    )(own, w_in, w_out)
    grads, more_act, more_dpre = pl.pallas_call(
        hidden_kernel,
        out_shape=(pltpu.HBM((zs, 2, 2, 4, 4, SLICE, SIDE), BF16), half, half),
        in_specs=[VMEM] * 6,
        out_specs=(HBM, VMEM, VMEM),
        scratch_shapes=[
            pltpu.VMEM((4, 4, zs, 2, 2, SLICE, SIDE), BF16),
            pltpu.SemaphoreType.DMA((4, 4)),
        ],
        compiler_params=params(),
        name="hidden",
    )(own, oth, first_act, first_dpre, w_in, w_out)

    columns = [[z * 2 + xl for z in range(zs)] for xl in range(2)]
    grad_sum = lax.psum_scatter(
        grads.reshape(-1, SIDE), "dp", scatter_dimension=0, axis_index_groups=columns, tiled=True
    )

    part_own, part_oth = pl.pallas_call(
        project_kernel,
        out_shape=(share, share),
        in_specs=[VMEM] * 6,
        out_specs=(VMEM, VMEM),
        compiler_params=params(),
        name="project",
    )(first_act, first_dpre, more_act, more_dpre, w_in, w_out)
    part_mate = lax.ppermute(part_oth, "mp", mate)
    part = (part_own.astype(F32) + part_mate.astype(F32)).astype(BF16)
    slices = lax.all_to_all(part, "mp", 0, 0, axis_index_groups=same_core, tiled=True)
    sorted_ = pl.pallas_call(
        sort_kernel,
        out_shape=jax.ShapeDtypeStruct((n, 2 * SLICE, 2 * SIDE), BF16),
        in_specs=[SMEM, VMEM],
        out_specs=VMEM,
        compiler_params=params(),
        name="sort",
    )(table, slices)
    final = lax.all_to_all(sorted_, "mp", 0, 0, tiled=True)
    output = final[:, :SLICE].reshape(tok, 2 * SIDE)
    grad_tokens = final[:, SLICE:].reshape(tok, 2 * SIDE)

    grad_sum, output, grad_tokens = lax.optimization_barrier((grad_sum, output, grad_tokens))
    halves = grad_sum.reshape(2, 2, 4, 4, SLICE, SIDE)
    summed = in_hbm(halves)
    part = (4, 4, SLICE, SIDE)
    fetch = lambda half, which, name: pl.pallas_call(
        functools.partial(fetch_kernel, half, which),
        out_shape=jax.ShapeDtypeStruct(part, BF16),
        in_specs=[HBM],
        out_specs=VMEM,
        scratch_shapes=[pltpu.SemaphoreType.DMA],
        compiler_params=params(),
        name=name,
    )(summed)
    across = [(i, i ^ 1) for i in range(n_dp)]
    came = [lax.ppermute(fetch(1, which, "fetch_away"), "dp", across) for which in range(2)]
    mine = [fetch(0, which, "fetch_own") for which in range(2)]
    grad_in, grad_out = [
        pl.pallas_call(
            functools.partial(finish_kernel, 1.0 / math.sqrt(total_tok)),
            out_shape=pltpu.HBM(part, F32),
            in_specs=[VMEM, VMEM],
            out_specs=HBM,
            scratch_shapes=[pltpu.VMEM(part, F32), pltpu.SemaphoreType.DMA],
            compiler_params=params(),
            name="finish",
        )(mine[which], came[which])
        for which in range(2)
    ]
    return output, grad_tokens, grad_in, grad_out


def solution(mesh):
    placed = (
        P("dp", "mp"),
        P("dp", "mp"),
        P("mp", None, None, None),
        P("mp", None, None, None),
        P("mp", None),
        P("mp", None),
    )
    return jax.shard_map(
        shards,
        mesh=mesh,
        in_specs=placed,
        out_specs=(
            P("dp", "mp"),
            P("dp", "mp"),
            P("mp", None, "dp", None),
            P("mp", None, "dp", None),
        ),
        check_vma=False,
    )
```

```python
import functools
import math

import jax
import jax.numpy as jnp
from jax import lax
from jax.experimental import pallas as pl
from jax.experimental.pallas import tpu as pltpu
from jax.sharding import PartitionSpec as P

SIDE = 256
QUAD = 4 * SIDE
SLICE = 16
LANES = 128
TILES = 2 * SIDE // LANES
VMEM = pl.BlockSpec(memory_space=pltpu.VMEM)
HBM = pl.BlockSpec(memory_space=pltpu.HBM)
SMEM = pl.BlockSpec(memory_space=pltpu.SMEM)
BF16 = jnp.bfloat16
F32 = jnp.float32


def in_hbm(array):
    return pltpu.with_memory_space_constraint(array, pltpu.HBM)


def params():
    return pltpu.CompilerParams(vmem_limit_bytes=40 * 1024 * 1024)


def pack_kernel(x_ref, dy_ref, p_ref, q_ref, out_ref, lists, sems):
    copies = [
        pltpu.make_async_copy(p_ref, lists.at[0], sems.at[0]),
        pltpu.make_async_copy(q_ref, lists.at[1], sems.at[1]),
    ]
    for part, ref in enumerate((x_ref, dy_ref)):
        for tile in range(TILES):
            at = part * TILES + tile
            source = ref.at[:, :, pl.ds(tile * LANES, LANES)]
            target = out_ref.at[:, pl.ds(at * SLICE, SLICE), :]
            copies.append(pltpu.make_async_copy(source, target, sems.at[2 + at]))
    for copy in copies:
        copy.start()
    row = lax.broadcasted_iota(jnp.int32, (4, LANES), 0)
    lane = lax.broadcasted_iota(jnp.int32, (4, LANES), 1)
    total = jnp.zeros((1, LANES), F32)
    for part in range(2):
        copies[part].wait()
        column = jnp.broadcast_to(lists[part][:, 0:1], (4, LANES)).astype(F32)
        total = total + jnp.sum(jnp.where(lane == row + 4 * part, column, 0.0), axis=0, keepdims=True)
    shape = (out_ref.shape[0], SLICE, LANES)
    out_ref[:, pl.ds(2 * TILES * SLICE, SLICE), :] = jnp.broadcast_to(total[None], shape).astype(BF16)
    for copy in copies[2:]:
        copy.wait()


def select_kernel(got_ref, out_ref, lists_ref):
    lists = jnp.max(got_ref[:, pl.ds(2 * TILES * SLICE, SLICE), :].astype(F32), axis=1).astype(jnp.int32)
    lists_ref[...] = lists
    chips = out_ref.shape[0]
    for group in range(chips // 2):
        for slot in range(8):
            for row, column in ((0, slot % 4), (SLICE, slot % 4 + 4)):
                block = lists[2 * group + slot // 4, column]
                owner = lax.shift_right_logical(block, 1)
                first = row * TILES + (block & 1) * (2 * SLICE)
                for tile in range(2):
                    rows = pl.ds(pl.multiple_of(first + tile * SLICE, SLICE), SLICE)
                    piece = got_ref[owner, rows, :]
                    lanes = pl.ds(tile * LANES, LANES)
                    out_ref[group, slot, pl.ds(row, SLICE), lanes] = piece
                    out_ref[group + chips // 2, slot, pl.ds(row, SLICE), lanes] = piece


def dot(a, b, da, db):
    return lax.dot_general(a, b, (((da,), (db,)), ((), ())), preferred_element_type=F32)


def slots_of(j):
    core = lax.axis_index("mp") & 1
    return [4 * core + (j ^ m) for m in (0, 1, 2)] + [4 * (1 - core) + j]


def block_of(ref, row, slot):
    return ref[:, slot, pl.ds(row, SLICE), :].reshape(-1, SIDE)


def activations(ref, win_ref, wout_ref, j):
    slots = slots_of(j)
    pre = sum(dot(block_of(ref, 0, slots[k]), win_ref[j, k], 1, 0) for k in range(4))
    d_act = sum(dot(block_of(ref, SLICE, slots[k]), wout_ref[j, k], 1, 1) for k in range(4))
    c = math.sqrt(2.0 / math.pi)
    square = pre * pre
    th = jnp.tanh(c * (pre + 0.044715 * (square * pre)))
    half = 0.5 * (1.0 + th)
    slope = half + (0.5 * c) * pre * (1.0 - th * th) * (1.0 + (3 * 0.044715) * square)
    return (pre * half).astype(BF16), (d_act * slope).astype(BF16)


def first_kernel(own_ref, win_ref, wout_ref, act_ref, dpre_ref):
    for j in range(4):
        lanes = pl.ds(j * SIDE, SIDE)
        act_ref[:, lanes], dpre_ref[:, lanes] = activations(own_ref, win_ref, wout_ref, j)


def hidden_kernel(
    own_ref, oth_ref, act_ref, dpre_ref, win_ref, wout_ref,
    grads_ref, more_act_ref, more_dpre_ref, held, sems,
):
    side = lax.axis_index("dp") & 1
    zs = held.shape[2]
    copies = []
    made = []
    for j in range(4):
        lanes = pl.ds(j * SIDE, SIDE)
        act, d_pre = activations(oth_ref, win_ref, wout_ref, j)
        more_act_ref[:, lanes] = act
        more_dpre_ref[:, lanes] = d_pre
        act = jnp.concatenate([act_ref[:, lanes], act], axis=0)
        made.append((act, jnp.concatenate([dpre_ref[:, lanes], d_pre], axis=0)))
    for j, (act, d_pre) in enumerate(made):
        for k, slot in enumerate(slots_of(j)):
            x = jnp.concatenate([block_of(own_ref, 0, slot), block_of(oth_ref, 0, slot)], axis=0)
            dy = jnp.concatenate([block_of(own_ref, SLICE, slot), block_of(oth_ref, SLICE, slot)], axis=0)
            g_in = dot(x, d_pre, 0, 0).astype(BF16).reshape(zs, 2, SLICE, SIDE)
            g_out = dot(act, dy, 0, 0).astype(BF16).reshape(zs, 2, SLICE, SIDE)
            for away in range(2):
                held[j, k, :, away ^ side, 0] = g_in[:, away]
                held[j, k, :, away ^ side, 1] = g_out[:, away]
            copies.append(pltpu.make_async_copy(held.at[j, k], grads_ref.at[:, :, :, j, k], sems.at[j, k]))
            copies[-1].start()
    for copy in copies:
        copy.wait()


def project_kernel(
    act_ref, dpre_ref, more_act_ref, more_dpre_ref, win_ref, wout_ref, own_ref, oth_ref
):
    core = lax.axis_index("mp") & 1

    def joined(first_ref, more_ref, t):
        lanes = pl.ds(t * SIDE, SIDE)
        return jnp.concatenate([first_ref[:, lanes], more_ref[:, lanes]], axis=0)

    acts = [joined(act_ref, more_act_ref, t) for t in range(4)]
    dpres = [joined(dpre_ref, more_dpre_ref, t) for t in range(4)]

    def put(row, slot, total):
        pieces = total.astype(BF16).reshape(2, -1, SLICE, SIDE)
        own_ref[:, slot, pl.ds(row, SLICE), :] = pieces[0]
        oth_ref[:, slot, pl.ds(row, SLICE), :] = pieces[1]

    for s in range(4):
        near, far = 4 * core + s, 4 * (1 - core) + s
        three = [(k, s ^ m) for k, m in enumerate((0, 1, 2))]
        put(0, near, sum(dot(acts[j], wout_ref[j, k], 1, 0) for k, j in three))
        put(0, far, dot(acts[s], wout_ref[s, 3], 1, 0))
        put(SLICE, near, sum(dot(dpres[j], win_ref[j, k], 1, 1) for k, j in three))
        put(SLICE, far, dot(dpres[s], win_ref[s, 3], 1, 1))


def sort_kernel(table, got_ref, out_ref):
    chips = got_ref.shape[0]
    for group in range(chips // 2):
        for slot in range(8):
            for row, column in ((0, slot % 4 + 4), (SLICE, slot % 4)):
                block = table[2 * group + slot // 4, column]
                owner = lax.shift_right_logical(block, 1)
                half = pl.multiple_of((block & 1) * SIDE, SIDE)
                rows = pl.ds(row, SLICE)
                total = got_ref[group, slot, rows, :].astype(F32)
                total = total + got_ref[group + chips // 2, slot, rows, :].astype(F32)
                out_ref[owner, rows, pl.ds(half, SIDE)] = total.astype(BF16)


def fetch_kernel(half, sum_ref, in_ref, out_ref, sems):
    copies = [
        pltpu.make_async_copy(sum_ref.at[half, which], ref, sems.at[which])
        for which, ref in enumerate((in_ref, out_ref))
    ]
    for copy in copies:
        copy.start()
    for copy in copies:
        copy.wait()


def finish_kernel(scale, own_ref, came_ref, out_ref, held, sem):
    held[...] = (own_ref[...].astype(F32) + came_ref[...].astype(F32)) * scale
    copy = pltpu.make_async_copy(held, out_ref, sem)
    copy.start()
    copy.wait()


def shards(tokens, cotangent, w_in, w_out, in_blocks, out_blocks):
    n = lax.axis_size("mp")
    n_dp = lax.axis_size("dp")
    zs = n_dp // 2
    tok = tokens.shape[0]
    total_tok = tok * n_dp
    mate = [(i, i ^ 1) for i in range(n)]
    same_core = [[2 * chip + core for chip in range(n // 2)] for core in range(2)]

    packed = pl.pallas_call(
        pack_kernel,
        out_shape=jax.ShapeDtypeStruct((n, (2 * TILES + 1) * SLICE, LANES), BF16),
        in_specs=[HBM] * 4,
        out_specs=VMEM,
        scratch_shapes=[pltpu.VMEM((2, 4, 4), jnp.int32), pltpu.SemaphoreType.DMA((2 + 2 * TILES,))],
        compiler_params=params(),
        name="pack",
    )(
        in_hbm(tokens.reshape(n, SLICE, 2 * SIDE)),
        in_hbm(cotangent.reshape(n, SLICE, 2 * SIDE)),
        in_hbm(in_blocks),
        in_hbm(out_blocks),
    )
    got = lax.all_to_all(packed, "mp", 0, 0, tiled=True)
    share = jax.ShapeDtypeStruct((n // 2, 8, 2 * SLICE, SIDE), BF16)
    chosen, table = pl.pallas_call(
        select_kernel,
        out_shape=(share, jax.ShapeDtypeStruct((n, LANES), jnp.int32)),
        in_specs=[VMEM],
        out_specs=(VMEM, VMEM),
        compiler_params=params(),
        name="select",
    )(got)
    own = lax.all_to_all(chosen, "mp", 0, 0, axis_index_groups=same_core, tiled=True)
    oth = lax.ppermute(own, "mp", mate)

    half = jax.ShapeDtypeStruct((tok // 2, QUAD), BF16)
    first_act, first_dpre = pl.pallas_call(
        first_kernel,
        out_shape=(half, half),
        in_specs=[VMEM] * 3,
        out_specs=(VMEM, VMEM),
        compiler_params=params(),
        name="first",
    )(own, w_in, w_out)
    grads, more_act, more_dpre = pl.pallas_call(
        hidden_kernel,
        out_shape=(pltpu.HBM((zs, 2, 2, 4, 4, SLICE, SIDE), BF16), half, half),
        in_specs=[VMEM] * 6,
        out_specs=(HBM, VMEM, VMEM),
        scratch_shapes=[
            pltpu.VMEM((4, 4, zs, 2, 2, SLICE, SIDE), BF16),
            pltpu.SemaphoreType.DMA((4, 4)),
        ],
        compiler_params=params(),
        name="hidden",
    )(own, oth, first_act, first_dpre, w_in, w_out)

    columns = [[z * 2 + xl for z in range(zs)] for xl in range(2)]
    grad_sum = lax.psum_scatter(
        grads.reshape(-1, SIDE), "dp", scatter_dimension=0, axis_index_groups=columns, tiled=True
    )

    part_own, part_oth = pl.pallas_call(
        project_kernel,
        out_shape=(share, share),
        in_specs=[VMEM] * 6,
        out_specs=(VMEM, VMEM),
        compiler_params=params(),
        name="project",
    )(first_act, first_dpre, more_act, more_dpre, w_in, w_out)
    part_mate = lax.ppermute(part_oth, "mp", mate)
    part = (part_own.astype(F32) + part_mate.astype(F32)).astype(BF16)
    slices = lax.all_to_all(part, "mp", 0, 0, axis_index_groups=same_core, tiled=True)
    sorted_ = pl.pallas_call(
        sort_kernel,
        out_shape=jax.ShapeDtypeStruct((n, 2 * SLICE, 2 * SIDE), BF16),
        in_specs=[SMEM, VMEM],
        out_specs=VMEM,
        compiler_params=params(),
        name="sort",
    )(table, slices)
    final = lax.all_to_all(sorted_, "mp", 0, 0, tiled=True)
    output = final[:, :SLICE].reshape(tok, 2 * SIDE)
    grad_tokens = final[:, SLICE:].reshape(tok, 2 * SIDE)

    grad_sum, output, grad_tokens = lax.optimization_barrier((grad_sum, output, grad_tokens))
    halves = grad_sum.reshape(2, 2, 4, 4, SLICE, SIDE)
    summed = in_hbm(halves)
    part = (4, 4, SLICE, SIDE)
    fetched = jax.ShapeDtypeStruct(part, BF16)
    fetch = lambda half, name: pl.pallas_call(
        functools.partial(fetch_kernel, half),
        out_shape=(fetched, fetched),
        in_specs=[HBM],
        out_specs=(VMEM, VMEM),
        scratch_shapes=[pltpu.SemaphoreType.DMA((2,))],
        compiler_params=params(),
        name=name,
    )(summed)
    across = [(i, i ^ 1) for i in range(n_dp)]
    came = [lax.ppermute(away, "dp", across) for away in fetch(1, "fetch_away")]
    mine = fetch(0, "fetch_own")
    grad_in, grad_out = [
        pl.pallas_call(
            functools.partial(finish_kernel, 1.0 / math.sqrt(total_tok)),
            out_shape=pltpu.HBM(part, F32),
            in_specs=[VMEM, VMEM],
            out_specs=HBM,
            scratch_shapes=[pltpu.VMEM(part, F32), pltpu.SemaphoreType.DMA],
            compiler_params=params(),
            name="finish",
        )(mine[which], came[which])
        for which in range(2)
    ]
    return output, grad_tokens, grad_in, grad_out


def solution(mesh):
    placed = (
        P("dp", "mp"),
        P("dp", "mp"),
        P("mp", None, None, None),
        P("mp", None, None, None),
        P("mp", None),
        P("mp", None),
    )
    return jax.shard_map(
        shards,
        mesh=mesh,
        in_specs=placed,
        out_specs=(
            P("dp", "mp"),
            P("dp", "mp"),
            P("mp", None, "dp", None),
            P("mp", None, "dp", None),
        ),
        check_vma=False,
    )
```

```python
import functools
import math

import jax
import jax.numpy as jnp
from jax import lax
from jax.experimental import pallas as pl
from jax.experimental.pallas import tpu as pltpu
from jax.sharding import PartitionSpec as P

SIDE = 256
QUAD = 4 * SIDE
SLICE = 16
LANES = 128
TILES = 2 * SIDE // LANES
VMEM = pl.BlockSpec(memory_space=pltpu.VMEM)
HBM = pl.BlockSpec(memory_space=pltpu.HBM)
SMEM = pl.BlockSpec(memory_space=pltpu.SMEM)
BF16 = jnp.bfloat16
F32 = jnp.float32


def in_hbm(array):
    return pltpu.with_memory_space_constraint(array, pltpu.HBM)


def params():
    return pltpu.CompilerParams(vmem_limit_bytes=40 * 1024 * 1024)


def pack_kernel(x_ref, dy_ref, p_ref, q_ref, out_ref, lists, sems):
    copies = [
        pltpu.make_async_copy(p_ref, lists.at[0], sems.at[0]),
        pltpu.make_async_copy(q_ref, lists.at[1], sems.at[1]),
    ]
    for part, ref in enumerate((x_ref, dy_ref)):
        for tile in range(TILES):
            at = part * TILES + tile
            source = ref.at[:, :, pl.ds(tile * LANES, LANES)]
            target = out_ref.at[:, pl.ds(at * SLICE, SLICE), :]
            copies.append(pltpu.make_async_copy(source, target, sems.at[2 + at]))
    for copy in copies:
        copy.start()
    row = lax.broadcasted_iota(jnp.int32, (4, LANES), 0)
    lane = lax.broadcasted_iota(jnp.int32, (4, LANES), 1)
    total = jnp.zeros((1, LANES), F32)
    for part in range(2):
        copies[part].wait()
        column = jnp.broadcast_to(lists[part][:, 0:1], (4, LANES)).astype(F32)
        total = total + jnp.sum(jnp.where(lane == row + 4 * part, column, 0.0), axis=0, keepdims=True)
    shape = (out_ref.shape[0], SLICE, LANES)
    out_ref[:, pl.ds(2 * TILES * SLICE, SLICE), :] = jnp.broadcast_to(total[None], shape).astype(BF16)
    for copy in copies[2:]:
        copy.wait()


def select_kernel(got_ref, out_ref, lists_ref):
    lists = got_ref[:, pl.ds(2 * TILES * SLICE, SLICE), :].astype(F32)[:, 0, :].astype(jnp.int32)
    lists_ref[...] = lists
    chips = out_ref.shape[0]
    for group in range(chips // 2):
        for slot in range(8):
            for row, column in ((0, slot % 4), (SLICE, slot % 4 + 4)):
                block = lists[2 * group + slot // 4, column]
                owner = lax.shift_right_logical(block, 1)
                first = row * TILES + (block & 1) * (2 * SLICE)
                for tile in range(2):
                    rows = pl.ds(pl.multiple_of(first + tile * SLICE, SLICE), SLICE)
                    piece = got_ref[owner, rows, :]
                    lanes = pl.ds(tile * LANES, LANES)
                    out_ref[group, slot, pl.ds(row, SLICE), lanes] = piece
                    out_ref[group + chips // 2, slot, pl.ds(row, SLICE), lanes] = piece


def dot(a, b, da, db):
    return lax.dot_general(a, b, (((da,), (db,)), ((), ())), preferred_element_type=F32)


def slots_of(j):
    core = lax.axis_index("mp") & 1
    return [4 * core + (j ^ m) for m in (0, 1, 2)] + [4 * (1 - core) + j]


def block_of(ref, row, slot):
    return ref[:, slot, pl.ds(row, SLICE), :].reshape(-1, SIDE)


def activations(ref, win_ref, wout_ref, j):
    slots = slots_of(j)
    pre = sum(dot(block_of(ref, 0, slots[k]), win_ref[j, k], 1, 0) for k in range(4))
    d_act = sum(dot(block_of(ref, SLICE, slots[k]), wout_ref[j, k], 1, 1) for k in range(4))
    c = math.sqrt(2.0 / math.pi)
    square = pre * pre
    th = jnp.tanh(c * (pre + 0.044715 * (square * pre)))
    half = 0.5 * (1.0 + th)
    slope = half + (0.5 * c) * pre * (1.0 - th * th) * (1.0 + (3 * 0.044715) * square)
    return (pre * half).astype(BF16), (d_act * slope).astype(BF16)


def first_kernel(own_ref, win_ref, wout_ref, act_ref, dpre_ref):
    for j in range(4):
        lanes = pl.ds(j * SIDE, SIDE)
        act_ref[:, lanes], dpre_ref[:, lanes] = activations(own_ref, win_ref, wout_ref, j)


def hidden_kernel(
    own_ref, oth_ref, act_ref, dpre_ref, win_ref, wout_ref,
    grads_ref, more_act_ref, more_dpre_ref, held, sems,
):
    side = lax.axis_index("dp") & 1
    zs = held.shape[3]
    copies = []
    made = []
    for j in range(4):
        lanes = pl.ds(j * SIDE, SIDE)
        act, d_pre = activations(oth_ref, win_ref, wout_ref, j)
        more_act_ref[:, lanes] = act
        more_dpre_ref[:, lanes] = d_pre
        act = jnp.concatenate([act_ref[:, lanes], act], axis=0)
        made.append((act, jnp.concatenate([dpre_ref[:, lanes], d_pre], axis=0)))
    for j, (act, d_pre) in enumerate(made):
        for k, slot in enumerate(slots_of(j)):
            x = jnp.concatenate([block_of(own_ref, 0, slot), block_of(oth_ref, 0, slot)], axis=0)
            dy = jnp.concatenate([block_of(own_ref, SLICE, slot), block_of(oth_ref, SLICE, slot)], axis=0)
            for which, (left, right) in enumerate(((x, d_pre), (act, dy))):
                grad = dot(left, right, 0, 0).astype(BF16).reshape(zs, 2, SLICE, SIDE)
                for away in range(2):
                    held[j, k, which, :, away ^ side] = grad[:, away]
                copies.append(
                    pltpu.make_async_copy(
                        held.at[j, k, which], grads_ref.at[:, :, which, j, k], sems.at[j, k, which]
                    )
                )
                copies[-1].start()
    for copy in copies:
        copy.wait()


def project_kernel(
    act_ref, dpre_ref, more_act_ref, more_dpre_ref, win_ref, wout_ref, own_ref, oth_ref
):
    core = lax.axis_index("mp") & 1

    def joined(first_ref, more_ref, t):
        lanes = pl.ds(t * SIDE, SIDE)
        return jnp.concatenate([first_ref[:, lanes], more_ref[:, lanes]], axis=0)

    acts = [joined(act_ref, more_act_ref, t) for t in range(4)]
    dpres = [joined(dpre_ref, more_dpre_ref, t) for t in range(4)]

    def put(row, slot, total):
        pieces = total.astype(BF16).reshape(2, -1, SLICE, SIDE)
        own_ref[:, slot, pl.ds(row, SLICE), :] = pieces[0]
        oth_ref[:, slot, pl.ds(row, SLICE), :] = pieces[1]

    for s in range(4):
        near, far = 4 * core + s, 4 * (1 - core) + s
        three = [(k, s ^ m) for k, m in enumerate((0, 1, 2))]
        put(0, near, sum(dot(acts[j], wout_ref[j, k], 1, 0) for k, j in three))
        put(0, far, dot(acts[s], wout_ref[s, 3], 1, 0))
        put(SLICE, near, sum(dot(dpres[j], win_ref[j, k], 1, 1) for k, j in three))
        put(SLICE, far, dot(dpres[s], win_ref[s, 3], 1, 1))


def sort_kernel(table, got_ref, out_ref):
    chips = got_ref.shape[0]
    for group in range(chips // 2):
        for slot in range(8):
            for row, column in ((0, slot % 4 + 4), (SLICE, slot % 4)):
                block = table[2 * group + slot // 4, column]
                owner = lax.shift_right_logical(block, 1)
                half = pl.multiple_of((block & 1) * SIDE, SIDE)
                rows = pl.ds(row, SLICE)
                total = got_ref[group, slot, rows, :].astype(F32)
                total = total + got_ref[group + chips // 2, slot, rows, :].astype(F32)
                out_ref[owner, rows, pl.ds(half, SIDE)] = total.astype(BF16)


def fetch_kernel(which, sum_ref, half_ref, sem):
    copy = pltpu.make_async_copy(sum_ref.at[which], half_ref, sem)
    copy.start()
    copy.wait()


def finish_kernel(scale, own_ref, came_ref, in_ref, out_ref, held, sems):
    copies = []
    for which, ref in enumerate((in_ref, out_ref)):
        held[which] = (own_ref[which].astype(F32) + came_ref[which].astype(F32)) * scale
        copies.append(pltpu.make_async_copy(held.at[which], ref, sems.at[which]))
        copies[-1].start()
    for copy in copies:
        copy.wait()


def shards(tokens, cotangent, w_in, w_out, in_blocks, out_blocks):
    n = lax.axis_size("mp")
    n_dp = lax.axis_size("dp")
    zs = n_dp // 2
    tok = tokens.shape[0]
    total_tok = tok * n_dp
    mate = [(i, i ^ 1) for i in range(n)]
    same_core = [[2 * chip + core for chip in range(n // 2)] for core in range(2)]

    packed = pl.pallas_call(
        pack_kernel,
        out_shape=jax.ShapeDtypeStruct((n, (2 * TILES + 1) * SLICE, LANES), BF16),
        in_specs=[HBM] * 4,
        out_specs=VMEM,
        scratch_shapes=[pltpu.VMEM((2, 4, 4), jnp.int32), pltpu.SemaphoreType.DMA((2 + 2 * TILES,))],
        compiler_params=params(),
        name="pack",
    )(
        in_hbm(tokens.reshape(n, SLICE, 2 * SIDE)),
        in_hbm(cotangent.reshape(n, SLICE, 2 * SIDE)),
        in_hbm(in_blocks),
        in_hbm(out_blocks),
    )
    got = lax.all_to_all(packed, "mp", 0, 0, tiled=True)
    share = jax.ShapeDtypeStruct((n // 2, 8, 2 * SLICE, SIDE), BF16)
    chosen, table = pl.pallas_call(
        select_kernel,
        out_shape=(share, jax.ShapeDtypeStruct((n, LANES), jnp.int32)),
        in_specs=[VMEM],
        out_specs=(VMEM, VMEM),
        compiler_params=params(),
        name="select",
    )(got)
    own = lax.all_to_all(chosen, "mp", 0, 0, axis_index_groups=same_core, tiled=True)
    oth = lax.ppermute(own, "mp", mate)

    half = jax.ShapeDtypeStruct((tok // 2, QUAD), BF16)
    first_act, first_dpre = pl.pallas_call(
        first_kernel,
        out_shape=(half, half),
        in_specs=[VMEM] * 3,
        out_specs=(VMEM, VMEM),
        compiler_params=params(),
        name="first",
    )(own, w_in, w_out)
    grads, more_act, more_dpre = pl.pallas_call(
        hidden_kernel,
        out_shape=(pltpu.HBM((zs, 2, 2, 4, 4, SLICE, SIDE), BF16), half, half),
        in_specs=[VMEM] * 6,
        out_specs=(HBM, VMEM, VMEM),
        scratch_shapes=[
            pltpu.VMEM((4, 4, 2, zs, 2, SLICE, SIDE), BF16),
            pltpu.SemaphoreType.DMA((4, 4, 2)),
        ],
        compiler_params=params(),
        name="hidden",
    )(own, oth, first_act, first_dpre, w_in, w_out)

    columns = [[z * 2 + xl for z in range(zs)] for xl in range(2)]
    grad_sum = lax.psum_scatter(
        grads.reshape(-1, SIDE), "dp", scatter_dimension=0, axis_index_groups=columns, tiled=True
    )

    part_own, part_oth = pl.pallas_call(
        project_kernel,
        out_shape=(share, share),
        in_specs=[VMEM] * 6,
        out_specs=(VMEM, VMEM),
        compiler_params=params(),
        name="project",
    )(first_act, first_dpre, more_act, more_dpre, w_in, w_out)
    part_mate = lax.ppermute(part_oth, "mp", mate)
    part = (part_own.astype(F32) + part_mate.astype(F32)).astype(BF16)
    slices = lax.all_to_all(part, "mp", 0, 0, axis_index_groups=same_core, tiled=True)
    sorted_ = pl.pallas_call(
        sort_kernel,
        out_shape=jax.ShapeDtypeStruct((n, 2 * SLICE, 2 * SIDE), BF16),
        in_specs=[SMEM, VMEM],
        out_specs=VMEM,
        compiler_params=params(),
        name="sort",
    )(table, slices)
    final = lax.all_to_all(sorted_, "mp", 0, 0, tiled=True)
    output = final[:, :SLICE].reshape(tok, 2 * SIDE)
    grad_tokens = final[:, SLICE:].reshape(tok, 2 * SIDE)

    grad_sum, output, grad_tokens = lax.optimization_barrier((grad_sum, output, grad_tokens))
    halves = grad_sum.reshape(2, 2, 4, 4, SLICE, SIDE)
    summed = in_hbm(halves)
    fetch = lambda which, name: pl.pallas_call(
        functools.partial(fetch_kernel, which),
        out_shape=jax.ShapeDtypeStruct((2, 4, 4, SLICE, SIDE), BF16),
        in_specs=[HBM],
        out_specs=VMEM,
        scratch_shapes=[pltpu.SemaphoreType.DMA],
        compiler_params=params(),
        name=name,
    )(summed)
    came = lax.ppermute(fetch(1, "fetch_away"), "dp", [(i, i ^ 1) for i in range(n_dp)])
    mine = fetch(0, "fetch_own")
    grad_shape = pltpu.HBM((4, 4, SLICE, SIDE), F32)
    grad_in, grad_out = pl.pallas_call(
        functools.partial(finish_kernel, 1.0 / math.sqrt(total_tok)),
        out_shape=(grad_shape, grad_shape),
        in_specs=[VMEM, VMEM],
        out_specs=(HBM, HBM),
        scratch_shapes=[
            pltpu.VMEM((2, 4, 4, SLICE, SIDE), F32),
            pltpu.SemaphoreType.DMA((2,)),
        ],
        compiler_params=params(),
        name="finish",
    )(mine, came)
    return output, grad_tokens, grad_in, grad_out


def solution(mesh):
    placed = (
        P("dp", "mp"),
        P("dp", "mp"),
        P("mp", None, None, None),
        P("mp", None, None, None),
        P("mp", None),
        P("mp", None),
    )
    return jax.shard_map(
        shards,
        mesh=mesh,
        in_specs=placed,
        out_specs=(
            P("dp", "mp"),
            P("dp", "mp"),
            P("mp", None, "dp", None),
            P("mp", None, "dp", None),
        ),
        check_vma=False,
    )
```
